256 devices in a mesh: loop: 32 (over z, y_lo, core), rep: 8 (over x, y_hi).
Axes of the slice: x: 4, y: 4 (y_hi: 2, y_lo: 2; y = y_hi * 2 + y_lo), z: 8, core: 2. Of those that a mesh axis runs over, the one named last changes fastest.
Arguments:
- node_features: bfloat16 [32768, 602], P('loop'), may hold values from -6 to 6
- weight: bfloat16 [602, 256], replicated, may hold values from -0.25 to 0.25
- degree: int32 [32768], P('loop'), may hold values from 4 to 47
- tile_index: int32 [32, 32, 32], P('loop', 'rep'), may hold values from 0 to 63, as said below
- edge_codes: int32 [32, 32, 32, 128], P('loop', 'rep'), may hold values from -1 to 16383, as said below
- cotangent: bfloat16 [32768, 256], P(('loop', 'rep')), may hold values from -6 to 6
Outputs:
- output: bfloat16 [32768, 256], P(('loop', 'rep'))
- grad_weight: float32 [602, 256], replicated
- grad_input: bfloat16 [32768, 602], P(('loop', 'rep'))
The draws below stay inside these ranges and needn't reach their ends.
Inputs may be any that keep to these rules, and one draw needn't show every extreme that they name: `tile_index`: in each pair of owner blocks, slot r * 4 + m lies in row tile r, and the 4 slots of one row tile name distinct column tiles. `edge_codes`: codes of one tile may repeat; the share of empty slots is set per owner and can differ between owners.
All inputs are finite; a program needn't handle non-finite values.
Results may differ from the reference program's by a relative error of at most 0.007.
Values may be sent and summed in bfloat16 or wider, within the bound.
A program may use at most 64 MiB of HBM per device.

```python
import math
import jax
import jax.numpy as jnp
from jax import lax

OWN = 1024
TILE = 128
ROW_TILES = 8
SLOTS_ROW = 4
SLOTS = 32
EPT = 128
F_IN = 602
HID = 256
NODES = 32768
N_LOOP = 32


def draw_tile_index(key, part):
    key = jax.random.fold_in(key, 11)
    shape = (N_LOOP, N_LOOP, ROW_TILES, ROW_TILES)
    scores = jax.random.randint(key, shape, 0, 65536, dtype=jnp.int32) * ROW_TILES
    scores = scores + jnp.arange(ROW_TILES, dtype=jnp.int32)
    order = jnp.argsort(scores, axis=-1, stable=True).astype(jnp.int32)
    chosen = order[..., :SLOTS_ROW]
    row_part = jnp.arange(ROW_TILES, dtype=jnp.int32)[:, None] * ROW_TILES
    return (row_part + chosen).reshape(N_LOOP, N_LOOP, SLOTS).astype(jnp.int32)


def draw_edge_codes(key, part):
    key = jax.random.fold_in(key, 23)
    level_key, live_key, code_key = jax.random.split(key, 3)
    shape = (N_LOOP, N_LOOP, SLOTS, EPT)
    level = jax.random.randint(level_key, (N_LOOP, 1, 1, 1), 1, 5, dtype=jnp.int32)
    draw_live = jax.random.randint(live_key, shape, 0, 4, dtype=jnp.int32)
    codes = jax.random.randint(code_key, shape, 0, TILE * TILE, dtype=jnp.int32)
    return jnp.where(draw_live < level, codes, -1).astype(jnp.int32)


def plant(values, key, low, high):
    extent = values.shape
    index_at = [jax.random.randint(jax.random.fold_in(key, axis), (), 0, extent[axis]) for axis in range(len(extent))]
    values = values.at[tuple(index_at)].set(low)
    longest = extent.index(max(extent))
    index_at[longest] = (index_at[longest] + 1) % extent[longest]
    return values.at[tuple(index_at)].set(high)


def block_levels(stream_key, dims, pieces, low, largest):
    def one(position, parts):
        draws = jax.random.uniform(jax.random.fold_in(jax.random.fold_in(stream_key, 6), position), (parts,), jnp.float32, low / len(pieces), largest / len(pieces))
        return jnp.repeat(jnp.exp(draws), dims[position] // parts).reshape((-1,) + (1,) * (len(dims) - position - 1))

    gain = one(*pieces[0])
    for cut in pieces[1:]:
        gain = gain * one(*cut)
    return gain


def scatter_about(key, shape, deviation, limit, cuts=(), kind=jnp.bfloat16):
    values = deviation * jax.random.normal(key, shape, jnp.float32)
    if cuts:
        values = values * block_levels(key, shape, cuts, -0.22, 0.18)
    return jnp.clip(values, -limit, limit).astype(kind)


def setup_inputs(seed: int = 0) -> dict:
    key_of = jax.random.split(jax.random.key(seed), 7)
    return {
        "node_features": scatter_about(key_of[0], (NODES, F_IN), 1.0, 6.0, ((0, 32),)),
        "weight": scatter_about(key_of[1], (F_IN, HID), F_IN ** -0.5, 0.25),
        "degree": plant(jax.random.randint(key_of[2], (NODES,), 4, 48), jax.random.fold_in(key_of[2], 1), 4, 47).astype(jnp.int32),
        "tile_index": draw_tile_index(jax.random.fold_in(key_of[6], 71), 0),
        "edge_codes": draw_edge_codes(jax.random.fold_in(key_of[6], 71), 0),
        "cotangent": scatter_about(key_of[5], (NODES, HID), 1.0, 6.0, ((0, 256),)),
    }


def block_coords(tile_row, code_row):
    clipped = jnp.maximum(code_row, 0)
    rows_local = (tile_row // ROW_TILES)[:, None] * TILE + clipped // TILE
    cols_local = (tile_row % ROW_TILES)[:, None] * TILE + clipped % TILE
    present = jnp.where(code_row >= 0, 1.0, 0.0).astype(jnp.float32)
    return (rows_local.reshape(-1).astype(jnp.int32), cols_local.reshape(-1).astype(jnp.int32), present.reshape(-1))

def spread_forward(scaled, tile_index, edge_codes):
    blocks = scaled.reshape(N_LOOP, OWN, HID)

    def per_owner(owner_index):

        def advance(running, offset):
            column = (owner_index - offset + N_LOOP) % N_LOOP
            source = blocks[column]
            rows_local, cols_local, present = block_coords(tile_index[owner_index, offset], edge_codes[owner_index, offset])
            values = source[cols_local] * present[:, None]
            return (running + jax.ops.segment_sum(values, rows_local, num_segments=OWN), None)
        start = jnp.zeros((OWN, HID), jnp.float32)
        return lax.scan(advance, start, jnp.arange(N_LOOP, dtype=jnp.int32))[0]
    return lax.map(per_owner, jnp.arange(N_LOOP, dtype=jnp.int32)).reshape(NODES, HID)

def spread_backward(upstream, tile_index, edge_codes):
    blocks = upstream.reshape(N_LOOP, OWN, HID)

    def per_target(target_index):

        def advance(running, offset):
            owner_index = (target_index + offset) % N_LOOP
            source = blocks[owner_index]
            rows_local, cols_local, present = block_coords(tile_index[owner_index, offset], edge_codes[owner_index, offset])
            values = source[rows_local] * present[:, None]
            return (running + jax.ops.segment_sum(values, cols_local, num_segments=OWN), None)
        start = jnp.zeros((OWN, HID), jnp.float32)
        return lax.scan(advance, start, jnp.arange(N_LOOP, dtype=jnp.int32))[0]
    return lax.map(per_target, jnp.arange(N_LOOP, dtype=jnp.int32)).reshape(NODES, HID)

def reference(node_features, weight, degree, tile_index, edge_codes, cotangent):
    inv_root = lax.rsqrt(degree.astype(jnp.float32))[:, None]
    proj = jnp.dot(node_features, weight, preferred_element_type=jnp.float32)
    scaled = (inv_root * proj).astype(jnp.bfloat16)
    scaled_wide = scaled.astype(jnp.float32)
    aggregate = spread_forward(scaled_wide, tile_index, edge_codes) + scaled_wide
    output = (inv_root * aggregate).astype(jnp.bfloat16)
    upstream = (inv_root * cotangent.astype(jnp.float32)).astype(jnp.bfloat16)
    upstream_wide = upstream.astype(jnp.float32)
    back = spread_backward(upstream_wide, tile_index, edge_codes) + upstream_wide
    node_grad = (inv_root * back).astype(jnp.bfloat16)
    grad_weight = jnp.dot(node_features.T, node_grad, preferred_element_type=jnp.float32) * (1.0 / math.sqrt(NODES))
    grad_input = jnp.dot(node_grad, weight.T, preferred_element_type=jnp.float32).astype(jnp.bfloat16)
    return (output, grad_weight, grad_input)
```

```python
import functools
import math

import jax
import jax.numpy as jnp
from jax import lax
from jax.experimental import pallas as pl
from jax.experimental.pallas import tpu as pltpu
from jax.sharding import PartitionSpec as P

MESH = pl.DeviceIdType.MESH
TILE = 128
HID = 256
OWN = 1024
F_IN = 602
F_PAD = 640
NZ = 8
F32 = jnp.float32
BF16 = jnp.bfloat16
VM = pl.BlockSpec(memory_space=pltpu.VMEM)
SM = pl.BlockSpec(memory_space=pltpu.SMEM)
VMEM_LIMIT = 56 * 1024 * 1024


def place():
    l = lax.axis_index("loop")
    r = lax.axis_index("rep")
    z, yl, k = l // 4, (l // 2) % 2, l % 2
    x, yh = r // 2, r % 2
    return z, yl, k, x, yh, r


def device(z, yl, k, r):
    return (z * 4 + yl * 2 + k, r)


def device_xy(z, k, x, y):
    return (z * 4 + (y % 2) * 2 + k, x * 2 + y // 2)


def remote(src, dst, send, recv, dev):
    return pltpu.make_async_remote_copy(
        src_ref=src, dst_ref=dst, send_sem=send, recv_sem=recv, device_id=dev, device_id_type=MESH
    )


def signal(sem, dev):
    pl.semaphore_signal(sem, inc=1, device_id=dev, device_id_type=MESH)


def gather_kernel(
    feat, weight, deg, cot, codes, tiles,
    xall, ut, got, ft, chunks, fpad,
    code_send, code_recv, u_send, u_recv, x_send, x_recv, f_send, f_recv,
):
    z, yl, k, x, yh, r = place()
    y = yh * 2 + yl
    q = yl * 2 + k
    mate = device(z, yl, 1 - k, r)
    y_up = device_xy(z, k, x, (y + 1) % 4)
    y_down = device_xy(z, k, x, (y + 3) % 4)

    barrier = pltpu.get_barrier_semaphore()
    signal(barrier, mate)
    signal(barrier, y_up)
    signal(barrier, y_down)

    def greet(i, carry):
        signal(barrier, device((z + i) % NZ, yl, k, r))
        return carry

    lax.fori_loop(1, NZ, greet, 0)

    def greet_sources(i, carry):
        zs, dz = i // 2, i % 2
        rs = (zs - z - dz + 2 * NZ) % NZ

        @pl.when(jnp.logical_not((zs == z) & (rs == r)))
        def _():
            signal(barrier, device(zs, yl, k, rs))

        return carry

    lax.fori_loop(0, 2 * NZ, greet_sources, 0)
    edge = jnp.where((r == 0) | (r == NZ - 1), 1, 0)

    for j in range(4):
        row = jnp.concatenate([tiles[j : j + 1, :], jnp.zeros((1, TILE - 32), jnp.int32)], axis=1)
        for t in range(8):
            chunks[t, j, 0:4, :] = codes[j, 4 * t : 4 * t + 4, :]
            chunks[t, j, 4:8, :] = jnp.broadcast_to(row, (4, TILE))

    root_rows = lax.rsqrt(deg[...].astype(F32))
    root_cols = root_rows.T
    own_root = lax.rsqrt(deg[pl.ds(r, 1), :].astype(F32))
    up = cot[...].astype(F32).T * own_root
    ut[z] = up.astype(BF16)

    pl.semaphore_wait(barrier, 26 - edge)

    def code_target(i):
        t, j = i // 4, i % 4
        zc = (z - r - jnp.where(j > q, 1, 0) + 2 * NZ) % NZ
        c4 = (q - j + 4) % 4
        return t, j, zc, c4

    def code_copy(i):
        t, j, zc, c4 = code_target(i)
        return remote(
            chunks.at[t, j], got.at[z, c4], code_send.at[i], code_recv.at[z * 4 + c4], device(zc, yl, k, t)
        )

    def send_codes(i, carry):
        t, j, zc, c4 = code_target(i)
        mine = (zc == z) & (t == r)

        @pl.when(mine)
        def _():
            got[z, c4] = chunks[t, j]

        @pl.when(jnp.logical_not(mine))
        def _():
            code_copy(i).start()

        return carry

    lax.fori_loop(0, 32, send_codes, 0)

    u_copies = []
    for d in (4, 3, 5, 2, 6, 1, 7):
        u_copies.append(
            remote(ut.at[z], ut.at[z], u_send.at[d], u_recv.at[d], device((z + d) % NZ, yl, k, r))
        )
        u_copies[-1].start()

    def project(first):
        for t in range(first, first + 4):
            rows = pl.ds(t * TILE, TILE)
            proj = jnp.dot(feat[rows, :], weight[...], preferred_element_type=F32)
            xall[q, rows, :] = (proj * root_cols[:, t : t + 1]).astype(BF16)

    low, high = pl.ds(0, 512), pl.ds(512, 512)
    project(0)
    x_up = remote(xall.at[q, low], xall.at[q, low], x_send.at[0], x_recv.at[0], y_up)
    x_up.start()
    project(4)
    x_down = remote(xall.at[q, high], xall.at[q, high], x_send.at[1], x_recv.at[1], y_down)
    x_down.start()
    x_mate = remote(xall.at[q], xall.at[q], x_send.at[2], x_recv.at[2], mate)
    x_mate.start()

    fpad[...] = jnp.zeros_like(fpad)
    fpad[:, 0:F_IN] = feat[pl.ds(pl.multiple_of(r * TILE, TILE), TILE), :]
    for b in range(F_PAD // TILE):
        block = fpad[:, b * TILE : (b + 1) * TILE].astype(F32)
        ft[k, b * TILE : (b + 1) * TILE, :] = block.T.astype(BF16)
    f_copy = remote(ft.at[k], ft.at[k], f_send, f_recv, mate)
    f_copy.start()

    other = (1 - yl) * 2 + k
    x_up.wait_recv()
    pass_low = remote(xall.at[other, low], xall.at[other, low], x_send.at[3], x_recv.at[3], mate)
    pass_low.start()
    x_down.wait_recv()
    pass_high = remote(xall.at[other, high], xall.at[other, high], x_send.at[4], x_recv.at[4], mate)
    pass_high.start()

    def wait_codes(i, carry):
        t, j, zc, c4 = code_target(i)

        @pl.when(jnp.logical_not((zc == z) & (t == r)))
        def _():
            code_copy(i).wait_send()

        zs, cs = i // 4, i % 4
        rs = ((4 * zs + q - 4 * z - cs + 64) % 32) // 4

        @pl.when(jnp.logical_not((zs == z) & (rs == r)))
        def _():
            remote(chunks.at[0, 0], got.at[zs, cs], code_send.at[i], code_recv.at[i], mate).wait_recv()

        return carry

    lax.fori_loop(0, 32, wait_codes, 0)
    for copy in u_copies:
        copy.wait()
    x_up.wait_send()
    x_down.wait_send()
    x_mate.wait()
    pass_low.wait()
    pass_high.wait()
    f_copy.wait()


def gather_call(feat, weight, deg, cot, codes, tiles):
    dma = pltpu.SemaphoreType.DMA
    return pl.pallas_call(
        gather_kernel,
        out_shape=(
            jax.ShapeDtypeStruct((4, OWN, HID), BF16),
            jax.ShapeDtypeStruct((NZ, HID, TILE), BF16),
            jax.ShapeDtypeStruct((NZ, 4, 8, TILE), jnp.int32),
            jax.ShapeDtypeStruct((2, F_PAD, TILE), BF16),
        ),
        in_specs=[VM] * 6,
        out_specs=(VM, VM, VM, VM),
        scratch_shapes=[
            pltpu.VMEM((8, 4, 8, TILE), jnp.int32),
            pltpu.VMEM((TILE, F_PAD), BF16),
            dma((32,)), dma((32,)), dma((8,)), dma((8,)), dma((5,)), dma((5,)), dma, dma,
        ],
        compiler_params=pltpu.CompilerParams(
            collective_id=0, has_side_effects=True, vmem_limit_bytes=VMEM_LIMIT
        ),
    )(feat, weight, deg, cot, codes, tiles)


def local_kernel(slots, got, xall, ut, bt, yout, tbuf, dense, utw):
    r = lax.axis_index("rep")
    lanes = lax.broadcasted_iota(jnp.int32, (TILE, TILE), 0)

    def build(i, carry):
        zs, c = i // 4, i % 4
        block = got[zs, c]
        for m in range(4):
            code = block[m : m + 1, :]
            rows = jnp.where(lanes == (code >> 7), 1.0, 0.0).astype(BF16)
            cols = jnp.where(lanes == (code & 127), 1.0, 0.0).astype(BF16)
            counts = lax.dot_general(rows, cols, (((1,), (1,)), ((), ())), preferred_element_type=F32)
            tbuf[i, m] = counts.astype(BF16)
        return carry

    lax.fori_loop(0, 32, build, 0, unroll=2)

    def fill(i, carry):
        zs, c = i // 4, i % 4
        spot = [slots[i, 4 * r + m] % 8 for m in range(4)]
        tbuf[i, 4] = jnp.zeros((TILE, TILE), BF16)
        for j in range(8):
            at = jnp.int32(4)
            for m in range(4):
                at = jnp.where(spot[m] == j, m, at)
            dense[c, pl.ds(pl.multiple_of(zs * TILE, TILE), TILE), j * TILE : (j + 1) * TILE] = tbuf[i, at]
        return carry

    lax.fori_loop(0, 32, fill, 0)
    for zs in range(NZ):
        utw[:, zs * TILE : (zs + 1) * TILE] = ut[zs]

    for c in range(4):
        ys, ks = c // 2, c % 2
        for xs in range(4):
            prod = jnp.dot(
                utw[...], dense[c, :, xs * 256 : (xs + 1) * 256], preferred_element_type=F32
            ).astype(BF16)
            for h in range(2):
                dest_y = 2 * h + ys
                piece = prod[:, h * TILE : (h + 1) * TILE]
                bt[ks, 0, xs, dest_y] = piece[0:TILE, :]
                bt[ks, 1, dest_y, xs] = piece[TILE:, :]

    def forward(i, carry):
        rows = pl.ds(pl.multiple_of(i * 256, 256), 256)
        total = jnp.dot(dense[0, rows, :], xall[0], preferred_element_type=F32)
        for c in range(1, 4):
            total = total + jnp.dot(dense[c, rows, :], xall[c], preferred_element_type=F32)
        yout[2 * i] = total[0:TILE].astype(BF16)
        yout[2 * i + 1] = total[TILE:].astype(BF16)
        return carry

    lax.fori_loop(0, 4, forward, 0)


def local_call(slots, got, xall, ut):
    return pl.pallas_call(
        local_kernel,
        out_shape=(
            jax.ShapeDtypeStruct((2, 2, 4, 4, TILE, TILE), BF16),
            jax.ShapeDtypeStruct((NZ, TILE, HID), BF16),
        ),
        in_specs=[SM, VM, VM, VM],
        out_specs=(VM, VM),
        scratch_shapes=[
            pltpu.VMEM((32, 5, TILE, TILE), BF16),
            pltpu.VMEM((4, OWN, OWN), BF16),
            pltpu.VMEM((HID, OWN), BF16),
        ],
        compiler_params=pltpu.CompilerParams(vmem_limit_bytes=VMEM_LIMIT),
    )(slots, got, xall, ut)


def reduce_kernel(
    scale, bt, ypart, xall, cot, deg, weight, ft,
    out, gin, gw,
    r_mate, s_part, r_one, p_part, r_two, r_fwd, ng, gpart, r_plane, r_z,
    m_send, m_recv, a_send, a_recv, b_send, b_recv, y_send, y_recv,
    n_send, n_recv, g_send, g_recv, z_send, z_recv, h_send, h_recv, e_send, e_recv,
):
    z, yl, k, x, yh, r = place()
    y = yh * 2 + yl
    q = yl * 2 + k
    mate = device(z, yl, 1 - k, r)
    spot = x * 4 + y

    barrier = pltpu.get_barrier_semaphore()
    signal(barrier, mate)

    def greet_z(i, carry):
        signal(barrier, device((z + i) % NZ, yl, k, r))
        return carry

    lax.fori_loop(1, NZ, greet_z, 0)

    def greet_plane(i, carry):
        signal(barrier, device_xy(z, k, (x + i // 4) % 4, (y + i) % 4))
        return carry

    lax.fori_loop(1, 16, greet_plane, 0)
    pl.semaphore_wait(barrier, 23)

    pending = []

    def send(src, dst, s, t, dev):
        copy = remote(src, dst, s, t, dev)
        copy.start()
        pending.append(copy)
        return copy

    order = (2, 1, 3, 0)
    here = (x, y)
    mates = {}
    for d in order:
        for h in range(2):
            at = (here[h] + d) % 4
            mates[h, d] = send(
                bt.at[1 - k, h, at], r_mate.at[h, at], m_send.at[h, d], m_recv.at[h, d], mate
            )
    fwd = [
        send(ypart.at[(z + d) % NZ], r_fwd.at[d], y_send.at[d], y_recv.at[d], device((z + d) % NZ, yl, k, r))
        for d in (4, 3, 5, 2, 6, 1, 7)
    ]

    ones = []
    for d in order:
        for h in range(2):
            at = (here[h] + d) % 4
            mates[h, d].wait_recv()
            s_part[h, at] = (bt[k, h, at].astype(F32) + r_mate[h, at].astype(F32)).astype(BF16)
            if d:
                dev = device_xy(z, k, (x + d) % 4, y) if h == 0 else device_xy(z, k, x, (y + d) % 4)
                ones.append(send(s_part.at[h, at], r_one.at[h, d], a_send.at[h, d], a_recv.at[h, d], dev))
    for copy in ones:
        copy.wait_recv()
    twos = []
    for d in order:
        for h in range(2):
            at = (here[1 - h] + d) % 4
            total = s_part[h, here[h], at].astype(F32)
            for e in range(1, 4):
                total = total + r_one[h, e, at].astype(F32)
            if d:
                p_part[h, d] = total.astype(BF16)
                dev = device_xy(z, k, x, (y + d) % 4) if h == 0 else device_xy(z, k, (x + d) % 4, y)
                twos.append(send(p_part.at[h, d], r_two.at[h, d], b_send.at[h, d], b_recv.at[h, d], dev))
            elif h == 0:
                top = total
            else:
                bottom = total

    for copy in twos:
        copy.wait_recv()
    for e in range(1, 4):
        top = top + r_two[0, e].astype(F32)
        bottom = bottom + r_two[1, e].astype(F32)
    own_root = lax.rsqrt(deg[pl.ds(r, 1), :].astype(F32))
    up = (cot[...].astype(F32).T * own_root).astype(BF16).astype(F32)
    back = jnp.concatenate([top, bottom], axis=0) + up
    node_grad = (back * own_root).astype(BF16).astype(F32)
    halves = (node_grad[0:TILE].T.astype(BF16), node_grad[TILE:].T.astype(BF16))

    @pl.when(k == 0)
    def _():
        ng[0, 0] = halves[0]
        ng[1, 0] = halves[1]

    @pl.when(k == 1)
    def _():
        ng[0, 1] = halves[0]
        ng[1, 1] = halves[1]

    swap = send(ng.at[1 - k, k], ng.at[1 - k, k], n_send, n_recv, mate)
    full = jnp.concatenate(halves, axis=1)
    gin[...] = lax.dot_general(
        full, weight[...], (((1,), (1,)), ((), ())), preferred_element_type=F32
    ).astype(BF16)
    swap.wait_recv()

    both_nodes = jnp.concatenate([ng[k, 0], ng[k, 1]], axis=0)
    both_feat = jnp.concatenate([ft[0], ft[1]], axis=1)
    gpart[...] = jnp.dot(both_feat, both_nodes, preferred_element_type=F32).reshape(16, F_PAD // 16, TILE)

    planes = []
    for i in (10, 9, 11, 6, 14, 2, 8, 5, 7, 13, 15, 1, 3, 4, 12):
        xs, ys = (x + i // 4) % 4, (y + i % 4) % 4
        planes.append(
            send(gpart.at[xs * 4 + ys], r_plane.at[i], g_send.at[i], g_recv.at[i], device_xy(z, k, xs, ys))
        )
    for copy in planes:
        copy.wait_recv()
    total = gpart[spot]
    for i in range(1, 16):
        total = total + r_plane[i]
    r_z[z] = total
    zs = []
    for d in (4, 3, 5, 2, 6, 1, 7):
        zs.append(send(r_z.at[z], r_z.at[z], z_send.at[d], z_recv.at[d], device((z + d) % NZ, yl, k, r)))
    for copy in zs:
        copy.wait_recv()
    total = r_z[0]
    for i in range(1, NZ):
        total = total + r_z[i]
    gw[k, spot] = total * scale
    spread = []
    for i in (10, 9, 11, 6, 14, 2, 8, 5, 7, 13, 15, 1, 3, 4, 12):
        xs, ys = (x + i // 4) % 4, (y + i % 4) % 4
        spread.append(
            send(gw.at[k, spot], gw.at[k, spot], h_send.at[i], h_recv.at[i], device_xy(z, k, xs, ys))
        )

    for copy in fwd:
        copy.wait_recv()
    rows = pl.ds(pl.multiple_of(r * TILE, TILE), TILE)
    total = ypart[z].astype(F32) + xall[q, rows, :].astype(F32)
    for d in range(1, NZ):
        total = total + r_fwd[d].astype(F32)
    root_col = jnp.broadcast_to(own_root, (8, TILE)).T
    out[...] = (total * root_col[:, 0:1]).astype(BF16)

    for copy in spread:
        copy.wait_recv()
    last = send(gw.at[k], gw.at[k], e_send, e_recv, mate)
    last.wait_recv()
    for copy in pending:
        copy.wait_send()


def reduce_call(scale, bt, ypart, xall, cot, deg, weight, ft):
    dma = pltpu.SemaphoreType.DMA
    chunk = F_PAD // 16
    return pl.pallas_call(
        functools.partial(reduce_kernel, scale),
        out_shape=(
            jax.ShapeDtypeStruct((TILE, HID), BF16),
            jax.ShapeDtypeStruct((TILE, F_IN), BF16),
            jax.ShapeDtypeStruct((2, 16, chunk, TILE), F32),
        ),
        in_specs=[VM] * 7,
        out_specs=(VM, VM, VM),
        scratch_shapes=[
            pltpu.VMEM((2, 4, 4, TILE, TILE), BF16),
            pltpu.VMEM((2, 4, 4, TILE, TILE), BF16),
            pltpu.VMEM((2, 4, 4, TILE, TILE), BF16),
            pltpu.VMEM((2, 4, TILE, TILE), BF16),
            pltpu.VMEM((2, 4, TILE, TILE), BF16),
            pltpu.VMEM((8, TILE, HID), BF16),
            pltpu.VMEM((2, 2, TILE, TILE), BF16),
            pltpu.VMEM((16, chunk, TILE), F32),
            pltpu.VMEM((16, chunk, TILE), F32),
            pltpu.VMEM((NZ, chunk, TILE), F32),
            dma((2, 4)), dma((2, 4)), dma((2, 4)), dma((2, 4)), dma((2, 4)), dma((2, 4)), dma((8,)), dma((8,)),
            dma, dma, dma((16,)), dma((16,)), dma((8,)), dma((8,)), dma((16,)), dma((16,)), dma, dma,
        ],
        compiler_params=pltpu.CompilerParams(
            collective_id=1, has_side_effects=True, vmem_limit_bytes=VMEM_LIMIT
        ),
    )(bt, ypart, xall, cot, deg, weight, ft)


def per_device(node_features, weight, degree, tile_index, edge_codes, cotangent):
    deg = degree.reshape(8, TILE)
    xall, ut, got, ft = gather_call(node_features, weight, deg, cotangent, edge_codes[0], tile_index[0])
    slots = got[:, :, 4, :].reshape(32, TILE)
    bt, ypart = local_call(slots, got, xall, ut)
    scale = 1.0 / math.sqrt(node_features.shape[0] * lax.axis_size("loop"))
    out, gin, gw = reduce_call(scale, bt, ypart, xall, cotangent, deg, weight, ft)
    gw = gw.reshape(2, F_PAD, TILE)
    grad_weight = jnp.concatenate([gw[0, :F_IN], gw[1, :F_IN]], axis=1)
    return (out, grad_weight, gin)


def solution(mesh):
    return jax.shard_map(
        per_device,
        mesh=mesh,
        in_specs=(
            P("loop", None),
            P(),
            P("loop"),
            P("loop", "rep", None),
            P("loop", "rep", None, None),
            P(("loop", "rep"), None),
        ),
        out_specs=(P(("loop", "rep"), None), P(), P(("loop", "rep"), None)),
        check_vma=False,
    )
```

```python
import functools
import math

import jax
import jax.numpy as jnp
from jax import lax
from jax.experimental import pallas as pl
from jax.experimental.pallas import tpu as pltpu
from jax.sharding import PartitionSpec as P

MESH = pl.DeviceIdType.MESH
TILE = 128
HID = 256
OWN = 1024
F_IN = 602
F_PAD = 640
CHUNK = F_PAD // 16
NZ = 8
F32 = jnp.float32
BF16 = jnp.bfloat16
VM = pl.BlockSpec(memory_space=pltpu.VMEM)
VMEM_LIMIT = 56 * 1024 * 1024
Z_ORDER = (4, 3, 5, 2, 6, 1, 7)
PLANE_ORDER = (10, 9, 11, 6, 14, 2, 8, 5, 7, 13, 15, 1, 3, 4, 12)
RING_ORDER = (2, 1, 3)


def device(z, yl, k, r):
    return (z * 4 + yl * 2 + k, r)


def device_xy(z, k, x, y):
    return (z * 4 + (y % 2) * 2 + k, x * 2 + y // 2)


def remote(src, dst, send, recv, dev):
    return pltpu.make_async_remote_copy(
        src_ref=src, dst_ref=dst, send_sem=send, recv_sem=recv, device_id=dev, device_id_type=MESH
    )


def signal(sem, dev):
    pl.semaphore_signal(sem, inc=1, device_id=dev, device_id_type=MESH)


def layer_kernel(
    scale, feat, weight, deg, cot, codes, tiles,
    out, gin, gw,
    chunks, got, spots, slots, tbuf, dense, xall, fother, dother, ut, utw, db,
    ymate, r_y, ys, r_fwd, bt, r_one, p_part, r_two, gp, r_swap, gs, r_plane, r_z,
    slot_sem, code_send, code_recv, u_send, u_recv, v_send, v_recv, x_send, x_recv, f_send, f_recv,
    m_send, m_recv, y_send, y_recv, a_send, a_recv, b_send, b_recv,
    w_send, w_recv, g_send, g_recv, z_send, z_recv, h_send, h_recv, e_send, e_recv,
):
    l = lax.axis_index("loop")
    r = lax.axis_index("rep")
    z, yl, k = l // 4, (l // 2) % 2, l % 2
    x, yh = r // 2, r % 2
    y = yh * 2 + yl
    spot = x * 4 + y
    mate = device(z, yl, 1 - k, r)
    y_up = device_xy(z, k, x, (y + 1) % 4)
    y_down = device_xy(z, k, x, (y + 3) % 4)

    def code_source(i):
        kr, zs, cr = i // 16, (i // 2) % 8, i % 2
        ks = (k + kr) % 2
        owner = 4 * zs + 2 * yl + ks
        column = 4 * z + 2 * ((yl + cr) % 2) + k
        rs = ((owner - column + 32) % 32) // 4
        return zs, ks, rs, (zs == z) & (ks == k) & (rs == r)

    def code_target(i):
        t, j = i // 4, i % 4
        column = (l - 4 * r - j + 64) % 32
        zc, yc, kc = column // 4, (column // 2) % 2, column % 2
        slot = ((k - kc + 2) % 2) * 16 + z * 2 + (yc - yl + 2) % 2
        return t, j, zc, kc, slot, (zc == z) & (kc == k) & (t == r)

    barrier = pltpu.get_barrier_semaphore()
    signal(barrier, mate)

    def greet_z(i, carry):
        signal(barrier, device((z + i) % NZ, yl, k, r))
        return carry

    lax.fori_loop(1, NZ, greet_z, 0)

    def greet_plane(i, carry):
        signal(barrier, device_xy(z, k, (x + i // 4) % 4, (y + i) % 4))
        return carry

    lax.fori_loop(1, 16, greet_plane, 0)

    def greet_sources(i, carry):
        zs, ks, rs, mine = code_source(i)

        @pl.when(jnp.logical_not(mine))
        def _():
            signal(barrier, device(zs, yl, ks, rs))

        return carry

    lax.fori_loop(0, 32, greet_sources, 0)
    kept = jnp.where(r == 0, 1 + yl, jnp.where(r == NZ - 1, 1 - yl, 0))

    for j in range(4):
        row = jnp.concatenate([tiles[j : j + 1, :], jnp.zeros((1, TILE - 32), jnp.int32)], axis=1)
        for t in range(8):
            chunks[t, j, 0:4, :] = codes[j, 4 * t : 4 * t + 4, :]
            chunks[t, j, 4:8, :] = jnp.broadcast_to(row, (4, TILE))

    root_rows = lax.rsqrt(deg[...].astype(F32))
    root_cols = root_rows.T
    own_root = lax.rsqrt(deg[pl.ds(r, 1), :].astype(F32))
    ut[z] = (cot[...].astype(F32).T * own_root).astype(BF16)
    for t in range(8):
        rows = slice(t * TILE, (t + 1) * TILE)
        proj = lax.dot_general(
            feat[:, rows], weight[...], (((0,), (0,)), ((), ())), preferred_element_type=F32
        )
        xall[0, rows, :] = (proj * root_cols[:, t : t + 1]).astype(BF16)

    pl.semaphore_wait(barrier, 55 - kept)

    pending = []

    def send(src, dst, s, t, dev):
        copy = remote(src, dst, s, t, dev)
        copy.start()
        pending.append(copy)
        return copy

    def send_codes(i, carry):
        t, j, zc, kc, slot, mine = code_target(i)

        @pl.when(mine)
        def _():
            got[slot] = chunks[t, j]

        @pl.when(jnp.logical_not(mine))
        def _():
            remote(
                chunks.at[t, j], got.at[slot], code_send.at[i], code_recv.at[slot], device(zc, yl, kc, t)
            ).start()

        return carry

    lax.fori_loop(0, 32, send_codes, 0)
    us = {
        d: send(ut.at[z], ut.at[z], u_send.at[d], u_recv.at[d], device((z + d) % NZ, yl, k, r)) for d in Z_ORDER
    }
    vs = [send(ut.at[z], ut.at[NZ + z], v_send.at[0], v_recv.at[0], mate)]
    low, high = pl.ds(0, 512), pl.ds(512, 512)
    xs = [
        send(xall.at[0, low], xall.at[1, low], x_send.at[0], x_recv.at[0], y_up),
        send(xall.at[0, high], xall.at[1, high], x_send.at[1], x_recv.at[1], y_down),
    ]
    fs = [
        send(deg, dother, f_send.at[2], f_recv.at[2], y_up),
        send(feat.at[:, low], fother.at[:, low], f_send.at[0], f_recv.at[0], y_up),
        send(feat.at[:, high], fother.at[:, high], f_send.at[1], f_recv.at[1], y_down),
    ]

    def wait_codes(i, carry):
        zs, ks, rs, mine = code_source(i)

        @pl.when(jnp.logical_not(mine))
        def _():
            remote(chunks.at[0, 0], got.at[i], code_send.at[i], code_recv.at[i], mate).wait_recv()

        return carry

    lax.fori_loop(0, 32, wait_codes, 0)

    spots[...] = got[:, 4, :]
    slot_copy = pltpu.make_async_copy(spots, slots, slot_sem)
    slot_copy.start()

    lanes = lax.broadcasted_iota(jnp.int32, (TILE, TILE), 0)

    def build(i, carry):
        block = got[i]
        for m in range(4):
            code = block[m : m + 1, :]
            rows = jnp.where(lanes == (code >> 7), 1.0, 0.0).astype(BF16)
            cols = jnp.where(lanes == (code & 127), 1.0, 0.0).astype(BF16)
            counts = lax.dot_general(rows, cols, (((1,), (1,)), ((), ())), preferred_element_type=F32)
            tbuf[i, m] = counts.astype(BF16)
        tbuf[i, 4] = jnp.zeros((TILE, TILE), BF16)
        return carry

    lax.fori_loop(0, 32, build, 0, unroll=2)
    slot_copy.wait()

    def fill(i, carry):
        w, c = i // 2, i % 2
        at_m = [slots[i, 4 * r + m] % 8 for m in range(4)]
        for j in range(8):
            at = jnp.int32(4)
            for m in range(4):
                at = jnp.where(at_m[m] == j, m, at)
            dense[c, pl.ds(pl.multiple_of(w * TILE, TILE), TILE), j * TILE : (j + 1) * TILE] = tbuf[i, at]
        return carry

    lax.fori_loop(0, 32, fill, 0)

    for copy in xs:
        copy.wait_recv()

    def forward(i, carry):
        rows = pl.ds(pl.multiple_of(OWN + i * 512, 512), 512)
        total = jnp.dot(dense[0, rows, :], xall[0], preferred_element_type=F32)
        total = total + jnp.dot(dense[1, rows, :], xall[1], preferred_element_type=F32)
        ymate[pl.ds(4 * i, 4)] = total.astype(BF16).reshape(4, TILE, HID)
        return carry

    lax.fori_loop(0, 2, forward, 0)
    swap_y = send(ymate, r_y, m_send, m_recv, mate)

    def forward_own(i, carry):
        rows = pl.ds(pl.multiple_of(i * 512, 512), 512)
        total = jnp.dot(dense[0, rows, :], xall[0], preferred_element_type=F32)
        total = total + jnp.dot(dense[1, rows, :], xall[1], preferred_element_type=F32)
        ys[pl.ds(4 * i, 4)] = total.astype(BF16).reshape(4, TILE, HID)
        return carry

    lax.fori_loop(0, 2, forward_own, 0)

    for d in (1, 7, 2, 6, 3, 5, 4):
        us[d].wait_recv()
        at = (z - d + NZ) % NZ
        vs.append(send(ut.at[at], ut.at[NZ + at], v_send.at[d], v_recv.at[d], mate))

    swap_y.wait_recv()
    for i in range(NZ):
        ys[i] = (ys[i].astype(F32) + r_y[i].astype(F32)).astype(BF16)
    fwd = [
        send(ys.at[(z + d) % NZ], r_fwd.at[d], y_send.at[d], y_recv.at[d], device((z + d) % NZ, yl, k, r))
        for d in Z_ORDER
    ]

    for copy in vs:
        copy.wait_recv()
    for i in range(2 * NZ):
        utw[:, i * TILE : (i + 1) * TILE] = ut[i]
    fs[0].wait_recv()
    other_rows = lax.rsqrt(dother[...].astype(F32))
    for c in range(2):
        ysd = (yl + c) % 2
        roots = root_rows if c == 0 else other_rows
        for xd in range(4):
            columns = slice(xd * 256, (xd + 1) * 256)
            prod = jnp.dot(utw[...], dense[c, :, columns], preferred_element_type=F32)
            root = jnp.concatenate([roots[2 * xd : 2 * xd + 1], roots[2 * xd + 1 : 2 * xd + 2]], axis=1)
            db[c, :, columns] = (prod * root).astype(BF16)
            prod = prod.astype(BF16)
            for h in range(2):
                piece = prod[:, h * TILE : (h + 1) * TILE]
                bt[0, xd, 2 * h + ysd] = piece[0:TILE, :]
                bt[1, 2 * h + ysd, xd] = piece[TILE:, :]

    up = (cot[...].astype(F32).T * own_root).astype(BF16).astype(F32)
    mine = pl.ds(pl.multiple_of(r * TILE, TILE), TILE)
    db[0, :, mine] = (db[0, :, mine].astype(F32) + up * own_root).astype(BF16)

    for copy in fs[1:]:
        copy.wait_recv()
    nt = (((1,), (1,)), ((), ()))
    part = lax.dot_general(feat[...], db[0], nt, preferred_element_type=F32)
    part = part + lax.dot_general(fother[...], db[1], nt, preferred_element_type=F32)
    for h in range(2):
        gp[h, 0:F_IN, :] = part[:, h * TILE : (h + 1) * TILE]
        gp[h, F_IN:F_PAD, :] = jnp.zeros((F_PAD - F_IN, TILE), F32)
    swap = send(gp.at[1 - k], r_swap, w_send, w_recv, mate)
    swap.wait_recv()
    gs[...] = (gp[k] + r_swap[...]).reshape(16, CHUNK, TILE)

    planes = []
    for i in PLANE_ORDER:
        xd, yd = (x + i // 4) % 4, (y + i % 4) % 4
        planes.append(
            send(gs.at[xd * 4 + yd], r_plane.at[i], g_send.at[i], g_recv.at[i], device_xy(z, k, xd, yd))
        )

    here = (x, y)
    ones = []
    for d in RING_ORDER:
        for h in range(2):
            at = (here[h] + d) % 4
            dev = device_xy(z, k, (x + d) % 4, y) if h == 0 else device_xy(z, k, x, (y + d) % 4)
            ones.append(send(bt.at[h, at], r_one.at[h, d], a_send.at[h, d], a_recv.at[h, d], dev))

    for copy in planes:
        copy.wait_recv()
    total = gs[spot]
    for i in range(1, 16):
        total = total + r_plane[i]
    r_z[z] = total
    zs = [
        send(r_z.at[z], r_z.at[z], z_send.at[d], z_recv.at[d], device((z + d) % NZ, yl, k, r)) for d in Z_ORDER
    ]

    for copy in ones:
        copy.wait_recv()
    twos = []
    for d in RING_ORDER + (0,):
        for h in range(2):
            at = (here[1 - h] + d) % 4
            total = bt[h, here[h], at].astype(F32)
            for e in range(1, 4):
                total = total + r_one[h, e, at].astype(F32)
            if d:
                p_part[h, d] = total.astype(BF16)
                dev = device_xy(z, k, x, (y + d) % 4) if h == 0 else device_xy(z, k, (x + d) % 4, y)
                twos.append(send(p_part.at[h, d], r_two.at[h, d], b_send.at[h, d], b_recv.at[h, d], dev))
            elif h == 0:
                top = total
            else:
                bottom = total

    for copy in zs:
        copy.wait_recv()
    total = r_z[0]
    for i in range(1, NZ):
        total = total + r_z[i]
    gw[k, spot] = total * scale
    spread = []
    for i in PLANE_ORDER:
        xd, yd = (x + i // 4) % 4, (y + i % 4) % 4
        spread.append(
            send(gw.at[k, spot], gw.at[k, spot], h_send.at[i], h_recv.at[i], device_xy(z, k, xd, yd))
        )

    for copy in twos:
        copy.wait_recv()
    for e in range(1, 4):
        top = top + r_two[0, e].astype(F32)
        bottom = bottom + r_two[1, e].astype(F32)
    back = jnp.concatenate([top, bottom], axis=0) + up
    node_grad = (back * own_root).astype(BF16)
    gin[...] = jnp.dot(weight[...], node_grad, preferred_element_type=F32).astype(BF16)

    for copy in fwd:
        copy.wait_recv()
    total = ys[z].astype(F32) + xall[0, mine, :].astype(F32)
    for d in range(1, NZ):
        total = total + r_fwd[d].astype(F32)
    root_col = jnp.broadcast_to(own_root, (8, TILE)).T
    out[...] = (total * root_col[:, 0:1]).astype(BF16)

    for copy in spread:
        copy.wait_recv()
    last = send(gw.at[k], gw.at[k], e_send, e_recv, mate)

    def wait_code_sends(i, carry):
        t, j, zc, kc, slot, mine = code_target(i)

        @pl.when(jnp.logical_not(mine))
        def _():
            remote(chunks.at[t, j], got.at[slot], code_send.at[i], code_recv.at[slot], mate).wait_send()

        return carry

    lax.fori_loop(0, 32, wait_code_sends, 0)
    last.wait_recv()
    for copy in pending:
        copy.wait_send()


def layer_call(scale, feat, weight, deg, cot, codes, tiles):
    dma = pltpu.SemaphoreType.DMA
    vm = pltpu.VMEM
    i32 = jnp.int32
    scratch = [
        vm((8, 4, 8, TILE), i32), vm((32, 8, TILE), i32), vm((32, TILE), i32), pltpu.SMEM((32, TILE), i32),
        vm((32, 5, TILE, TILE), BF16), vm((2, 2 * OWN, OWN), BF16), vm((2, OWN, HID), BF16),
        vm((F_IN, OWN), BF16), vm((8, TILE), i32), vm((2 * NZ, HID, TILE), BF16),
        vm((HID, 2 * OWN), BF16), vm((2, HID, OWN), BF16),
        vm((NZ, TILE, HID), BF16), vm((NZ, TILE, HID), BF16), vm((NZ, TILE, HID), BF16), vm((NZ, TILE, HID), BF16),
        vm((2, 4, 4, TILE, TILE), BF16), vm((2, 4, 4, TILE, TILE), BF16),
        vm((2, 4, TILE, TILE), BF16), vm((2, 4, TILE, TILE), BF16),
        vm((2, F_PAD, TILE), F32), vm((F_PAD, TILE), F32), vm((16, CHUNK, TILE), F32), vm((16, CHUNK, TILE), F32),
        vm((NZ, CHUNK, TILE), F32),
        dma, dma((32,)), dma((32,)), dma((8,)), dma((8,)), dma((8,)), dma((8,)), dma((2,)), dma((2,)), dma((3,)), dma((3,)),
        dma, dma, dma((8,)), dma((8,)), dma((2, 4)), dma((2, 4)), dma((2, 4)), dma((2, 4)),
        dma, dma, dma((16,)), dma((16,)), dma((8,)), dma((8,)), dma((16,)), dma((16,)), dma, dma,
    ]
    return pl.pallas_call(
        functools.partial(layer_kernel, scale),
        out_shape=(
            jax.ShapeDtypeStruct((TILE, HID), BF16),
            jax.ShapeDtypeStruct((F_IN, TILE), BF16),
            jax.ShapeDtypeStruct((2, 16, CHUNK, TILE), F32),
        ),
        in_specs=[VM] * 6,
        out_specs=(VM, VM, VM),
        scratch_shapes=scratch,
        compiler_params=pltpu.CompilerParams(
            collective_id=0, has_side_effects=True, vmem_limit_bytes=VMEM_LIMIT
        ),
    )(feat, weight, deg, cot, codes, tiles)


def per_device(node_features, weight, degree, tile_index, edge_codes, cotangent):
    scale = 1.0 / math.sqrt(node_features.shape[0] * lax.axis_size("loop"))
    out, gin, gw = layer_call(
        scale, node_features.T, weight, degree.reshape(8, TILE), cotangent, edge_codes[0], tile_index[0]
    )
    gw = gw.reshape(2, F_PAD, TILE)
    grad_weight = jnp.concatenate([gw[0, :F_IN], gw[1, :F_IN]], axis=1)
    return (out, grad_weight, gin.T)


def solution(mesh):
    return jax.shard_map(
        per_device,
        mesh=mesh,
        in_specs=(
            P("loop", None),
            P(),
            P("loop"),
            P("loop", "rep", None),
            P("loop", "rep", None, None),
            P(("loop", "rep"), None),
        ),
        out_specs=(P(("loop", "rep"), None), P(), P(("loop", "rep"), None)),
        check_vma=False,
    )
```

```python
import functools
import math

import jax
import jax.numpy as jnp
from jax import lax
from jax.experimental import pallas as pl
from jax.experimental.pallas import tpu as pltpu
from jax.sharding import PartitionSpec as P

MESH = pl.DeviceIdType.MESH
TILE = 128
HID = 256
OWN = 1024
F_IN = 602
F_PAD = 640
CHUNK = F_PAD // 16
NZ = 8
F32 = jnp.float32
BF16 = jnp.bfloat16
VM = pl.BlockSpec(memory_space=pltpu.VMEM)
VMEM_LIMIT = 56 * 1024 * 1024
Z_ORDER = (4, 3, 5, 2, 6, 1, 7)
PLANE_ORDER = (10, 9, 11, 6, 14, 2, 8, 5, 7, 13, 15, 1, 3, 4, 12)
RING_ORDER = (2, 1, 3)


def device(z, yl, k, r):
    return (z * 4 + yl * 2 + k, r)


def device_xy(z, k, x, y):
    return (z * 4 + (y % 2) * 2 + k, x * 2 + y // 2)


def remote(src, dst, send, recv, dev):
    return pltpu.make_async_remote_copy(
        src_ref=src, dst_ref=dst, send_sem=send, recv_sem=recv, device_id=dev, device_id_type=MESH
    )


def signal(sem, dev):
    pl.semaphore_signal(sem, inc=1, device_id=dev, device_id_type=MESH)


def layer_kernel(
    scale, feat, weight, deg, cot, codes, tiles,
    out, gin, gw,
    pairs, relay, chunks, got, spots, slots, tbuf, dense, xall, fother, dother, ut, utw, db,
    ymate, r_y, ys, r_fwd, bt, r_one, p_part, r_two, gp, r_swap, gs, r_plane, r_z,
    slot_sem, code_send, code_recv, c_send, c_recv, q_send, q_recv, u_send, u_recv, v_send, v_recv, x_send, x_recv, f_send, f_recv,
    m_send, m_recv, y_send, y_recv, a_send, a_recv, b_send, b_recv,
    w_send, w_recv, g_send, g_recv, z_send, z_recv, h_send, h_recv, e_send, e_recv,
):
    l = lax.axis_index("loop")
    r = lax.axis_index("rep")
    z, yl, k = l // 4, (l // 2) % 2, l % 2
    x, yh = r // 2, r % 2
    y = yh * 2 + yl
    spot = x * 4 + y
    mate = device(z, yl, 1 - k, r)
    y_up = device_xy(z, k, x, (y + 1) % 4)
    y_down = device_xy(z, k, x, (y + 3) % 4)

    def code_source(i, rs):
        ks, yc = (k + i // 2) % 2, (yl + i % 2) % 2
        zs = (z + rs + jnp.where(2 * yl + ks - 2 * yc - k < 0, 1, 0)) % NZ
        return zs, ks, (zs == z) & (ks == k)

    def code_target(j):
        column = (l - 4 * r - j + 64) % 32
        zc, yc, kc = column // 4, (column // 2) % 2, column % 2
        slot = ((k - kc + 2) % 2) * 2 + (yc - yl + 2) % 2
        return zc, kc, slot, (zc == z) & (kc == k)

    barrier = pltpu.get_barrier_semaphore()
    signal(barrier, mate)

    def greet_z(i, carry):
        signal(barrier, device((z + i) % NZ, yl, k, r))
        return carry

    lax.fori_loop(1, NZ, greet_z, 0)

    def greet_plane(i, carry):
        signal(barrier, device_xy(z, k, (x + i // 4) % 4, (y + i) % 4))
        return carry

    lax.fori_loop(1, 16, greet_plane, 0)

    for i in range(4):
        zs, ks, mine = code_source(i, r)

        @pl.when(jnp.logical_not(mine))
        def _():
            signal(barrier, device(zs, yl, ks, r))

    kept = jnp.where(r == 0, 1 + yl, jnp.where(r == NZ - 1, 1 - yl, 0))

    for j in range(4):
        row = jnp.concatenate([tiles[j : j + 1, :], jnp.zeros((1, TILE - 32), jnp.int32)], axis=1)
        pairs[j, 0:32, :] = codes[j]
        pairs[j, 32:40, :] = jnp.broadcast_to(row, (8, TILE))

    root_rows = lax.rsqrt(deg[...].astype(F32))
    root_cols = root_rows.T
    own_root = lax.rsqrt(deg[pl.ds(r, 1), :].astype(F32))
    ut[z] = (cot[...].astype(F32).T * own_root).astype(BF16)
    for t in range(8):
        rows = slice(t * TILE, (t + 1) * TILE)
        proj = lax.dot_general(
            feat[:, rows], weight[...], (((0,), (0,)), ((), ())), preferred_element_type=F32
        )
        xall[0, rows, :] = (proj * root_cols[:, t : t + 1]).astype(BF16)

    pl.semaphore_wait(barrier, 27 - kept)

    pending = []

    def send(src, dst, s, t, dev):
        copy = remote(src, dst, s, t, dev)
        copy.start()
        pending.append(copy)
        return copy

    def code_copy(j):
        zc, kc, slot, mine = code_target(j)
        copy = remote(pairs.at[j], relay.at[slot], code_send.at[j], code_recv.at[slot], device(zc, yl, kc, r))
        return slot, mine, copy

    for j in range(4):
        slot, mine, copy = code_copy(j)

        @pl.when(mine)
        def _():
            relay[slot] = pairs[j]

        @pl.when(jnp.logical_not(mine))
        def _():
            copy.start()

    quarter = pl.ds(pl.multiple_of(512 + x * TILE, TILE), TILE)
    y_quarter = device_xy(z, k, x, (y + 1 + 2 * (x % 2)) % 4)
    f_quarter = send(feat.at[:, quarter], fother.at[:, quarter], f_send.at[3], f_recv.at[3], y_quarter)
    us = {
        d: send(ut.at[z], ut.at[z], u_send.at[d], u_recv.at[d], device((z + d) % NZ, yl, k, r)) for d in Z_ORDER
    }
    vs = [send(ut.at[z], ut.at[NZ + z], v_send.at[0], v_recv.at[0], mate)]
    low, high = pl.ds(0, 512), pl.ds(512, 512)
    xs = [
        send(xall.at[0, low], xall.at[1, low], x_send.at[0], x_recv.at[0], y_up),
        send(xall.at[0, high], xall.at[1, high], x_send.at[1], x_recv.at[1], y_down),
    ]
    f_low, f_high = pl.ds(0, 256), pl.ds(256, 256)
    fs = [
        send(deg, dother, f_send.at[2], f_recv.at[2], y_up),
        send(feat.at[:, f_low], fother.at[:, f_low], f_send.at[0], f_recv.at[0], y_up),
        send(feat.at[:, f_high], fother.at[:, f_high], f_send.at[1], f_recv.at[1], y_down),
    ]

    for i in range(4):
        zs, ks, mine = code_source(i, r)

        @pl.when(jnp.logical_not(mine))
        def _():
            remote(pairs.at[0], relay.at[i], code_send.at[i], code_recv.at[i], mate).wait_recv()

    for i in range(4):
        for t in range(8):
            chunks[t, i, 0:4, :] = relay[i, 4 * t : 4 * t + 4, :]
            chunks[t, i, 4:8, :] = relay[i, 32:36, :]
    cs = []
    for d in (3, 5, 1, 7, 2, 6, 4):
        t = (r + d) % 8
        cs.append(send(chunks.at[t], got.at[pl.ds(4 * r, 4)], c_send.at[d], c_recv.at[d], (l, t)))
    got[pl.ds(4 * r, 4)] = chunks[r]
    f_quarter.wait_recv()
    for d in RING_ORDER:
        fs.append(
            send(
                fother.at[:, quarter], fother.at[:, quarter], q_send.at[d], q_recv.at[d],
                device_xy(z, k, (x + d) % 4, y),
            )
        )
    for copy in cs:
        copy.wait_recv()

    spots[...] = got[:, 4, :]
    slot_copy = pltpu.make_async_copy(spots, slots, slot_sem)
    slot_copy.start()

    lanes = lax.broadcasted_iota(jnp.int32, (TILE, TILE), 0)

    def build(i, carry):
        block = got[i]
        for m in range(4):
            code = block[m : m + 1, :]
            rows = jnp.where(lanes == (code >> 7), 1.0, 0.0).astype(BF16)
            cols = jnp.where(lanes == (code & 127), 1.0, 0.0).astype(BF16)
            counts = lax.dot_general(rows, cols, (((1,), (1,)), ((), ())), preferred_element_type=F32)
            tbuf[i, m] = counts.astype(BF16)
        tbuf[i, 4] = jnp.zeros((TILE, TILE), BF16)
        return carry

    lax.fori_loop(0, 32, build, 0, unroll=4)
    slot_copy.wait()

    def fill(i, carry):
        zs, _, _ = code_source(i % 4, i // 4)
        w, c = ((i // 2) % 2) * NZ + zs, i % 2
        at_m = [slots[i, 4 * r + m] % 8 for m in range(4)]
        for j in range(8):
            at = jnp.int32(4)
            for m in range(4):
                at = jnp.where(at_m[m] == j, m, at)
            dense[c, pl.ds(pl.multiple_of(w * TILE, TILE), TILE), j * TILE : (j + 1) * TILE] = tbuf[i, at]
        return carry

    lax.fori_loop(0, 32, fill, 0)

    for d in (1, 7, 2, 6, 3, 5, 4):
        us[d].wait_recv()
        at = (z - d + NZ) % NZ
        vs.append(send(ut.at[at], ut.at[NZ + at], v_send.at[d], v_recv.at[d], mate))

    for copy in vs:
        copy.wait_recv()
    for i in range(2 * NZ):
        utw[:, i * TILE : (i + 1) * TILE] = ut[i]
    fs[0].wait_recv()
    other_rows = lax.rsqrt(dother[...].astype(F32))
    for c in range(2):
        ysd = (yl + c) % 2
        roots = root_rows if c == 0 else other_rows
        for xd in range(4):
            columns = slice(xd * 256, (xd + 1) * 256)
            prod = jnp.dot(utw[...], dense[c, :, columns], preferred_element_type=F32)
            root = jnp.concatenate([roots[2 * xd : 2 * xd + 1], roots[2 * xd + 1 : 2 * xd + 2]], axis=1)
            db[c, :, columns] = (prod * root).astype(BF16)
            prod = prod.astype(BF16)
            for h in range(2):
                piece = prod[:, h * TILE : (h + 1) * TILE]
                bt[0, xd, 2 * h + ysd] = piece[0:TILE, :]
                bt[1, 2 * h + ysd, xd] = piece[TILE:, :]

    up = (cot[...].astype(F32).T * own_root).astype(BF16).astype(F32)
    mine = pl.ds(pl.multiple_of(r * TILE, TILE), TILE)
    db[0, :, mine] = (db[0, :, mine].astype(F32) + up * own_root).astype(BF16)

    for copy in fs[1:]:
        copy.wait_recv()
    nt = (((1,), (1,)), ((), ()))
    part = lax.dot_general(feat[...], db[0], nt, preferred_element_type=F32)
    part = part + lax.dot_general(fother[...], db[1], nt, preferred_element_type=F32)
    for h in range(2):
        gp[h, 0:F_IN, :] = part[:, h * TILE : (h + 1) * TILE]
        gp[h, F_IN:F_PAD, :] = jnp.zeros((F_PAD - F_IN, TILE), F32)
    swap = send(gp.at[1 - k], r_swap, w_send, w_recv, mate)
    swap.wait_recv()
    gs[...] = (gp[k] + r_swap[...]).reshape(16, CHUNK, TILE)

    planes = []
    for i in PLANE_ORDER:
        xd, yd = (x + i // 4) % 4, (y + i % 4) % 4
        planes.append(
            send(gs.at[xd * 4 + yd], r_plane.at[i], g_send.at[i], g_recv.at[i], device_xy(z, k, xd, yd))
        )

    here = (x, y)
    ones = []
    for d in RING_ORDER:
        for h in range(2):
            at = (here[h] + d) % 4
            dev = device_xy(z, k, (x + d) % 4, y) if h == 0 else device_xy(z, k, x, (y + d) % 4)
            ones.append(send(bt.at[h, at], r_one.at[h, d], a_send.at[h, d], a_recv.at[h, d], dev))

    for copy in xs:
        copy.wait_recv()

    def forward(i, carry):
        rows = pl.ds(pl.multiple_of(OWN + i * 512, 512), 512)
        total = jnp.dot(dense[0, rows, :], xall[0], preferred_element_type=F32)
        total = total + jnp.dot(dense[1, rows, :], xall[1], preferred_element_type=F32)
        ymate[pl.ds(4 * i, 4)] = total.astype(BF16).reshape(4, TILE, HID)
        return carry

    lax.fori_loop(0, 2, forward, 0)
    swap_y = send(ymate, r_y, m_send, m_recv, mate)

    def forward_own(i, carry):
        rows = pl.ds(pl.multiple_of(i * 512, 512), 512)
        total = jnp.dot(dense[0, rows, :], xall[0], preferred_element_type=F32)
        total = total + jnp.dot(dense[1, rows, :], xall[1], preferred_element_type=F32)
        ys[pl.ds(4 * i, 4)] = total.astype(BF16).reshape(4, TILE, HID)
        return carry

    lax.fori_loop(0, 2, forward_own, 0)

    swap_y.wait_recv()
    for i in range(NZ):
        ys[i] = (ys[i].astype(F32) + r_y[i].astype(F32)).astype(BF16)
    fwd = [
        send(ys.at[(z + d) % NZ], r_fwd.at[d], y_send.at[d], y_recv.at[d], device((z + d) % NZ, yl, k, r))
        for d in Z_ORDER
    ]

    for copy in planes:
        copy.wait_recv()
    total = gs[spot]
    for i in range(1, 16):
        total = total + r_plane[i]
    r_z[z] = total
    zs = [
        send(r_z.at[z], r_z.at[z], z_send.at[d], z_recv.at[d], device((z + d) % NZ, yl, k, r)) for d in Z_ORDER
    ]

    for copy in ones:
        copy.wait_recv()
    twos = []
    for d in RING_ORDER + (0,):
        for h in range(2):
            at = (here[1 - h] + d) % 4
            total = bt[h, here[h], at].astype(F32)
            for e in range(1, 4):
                total = total + r_one[h, e, at].astype(F32)
            if d:
                p_part[h, d] = total.astype(BF16)
                dev = device_xy(z, k, x, (y + d) % 4) if h == 0 else device_xy(z, k, (x + d) % 4, y)
                twos.append(send(p_part.at[h, d], r_two.at[h, d], b_send.at[h, d], b_recv.at[h, d], dev))
            elif h == 0:
                top = total
            else:
                bottom = total

    for copy in zs:
        copy.wait_recv()
    total = r_z[0]
    for i in range(1, NZ):
        total = total + r_z[i]
    half = pl.ds(pl.multiple_of(k * TILE, TILE), TILE)
    gw[spot, :, half] = total * scale
    spread = []
    for i in PLANE_ORDER:
        xd, yd = (x + i // 4) % 4, (y + i % 4) % 4
        spread.append(
            send(gw.at[spot, :, half], gw.at[spot, :, half], h_send.at[i], h_recv.at[i], device_xy(z, k, xd, yd))
        )

    for copy in twos:
        copy.wait_recv()
    for e in range(1, 4):
        top = top + r_two[0, e].astype(F32)
        bottom = bottom + r_two[1, e].astype(F32)
    back = jnp.concatenate([top, bottom], axis=0) + up
    node_grad = (back * own_root).astype(BF16)
    gin[...] = jnp.dot(weight[...], node_grad, preferred_element_type=F32).astype(BF16)

    for copy in fwd:
        copy.wait_recv()
    total = ys[z].astype(F32) + xall[0, mine, :].astype(F32)
    for d in range(1, NZ):
        total = total + r_fwd[d].astype(F32)
    root_col = jnp.broadcast_to(own_root, (8, TILE)).T
    out[...] = (total * root_col[:, 0:1]).astype(BF16)

    for copy in spread:
        copy.wait_recv()
    last = send(gw.at[:, :, half], gw.at[:, :, half], e_send, e_recv, mate)

    for j in range(4):
        _, mine, copy = code_copy(j)

        @pl.when(jnp.logical_not(mine))
        def _():
            copy.wait_send()

    last.wait_recv()
    for copy in pending:
        copy.wait_send()


def layer_call(scale, feat, weight, deg, cot, codes, tiles):
    dma = pltpu.SemaphoreType.DMA
    vm = pltpu.VMEM
    i32 = jnp.int32
    scratch = [
        vm((4, 40, TILE), i32), vm((4, 40, TILE), i32), vm((8, 4, 8, TILE), i32), vm((32, 8, TILE), i32), vm((32, TILE), i32), pltpu.SMEM((32, TILE), i32),
        vm((32, 5, TILE, TILE), BF16), vm((2, 2 * OWN, OWN), BF16), vm((2, OWN, HID), BF16),
        vm((F_IN, OWN), BF16), vm((8, TILE), i32), vm((2 * NZ, HID, TILE), BF16),
        vm((HID, 2 * OWN), BF16), vm((2, HID, OWN), BF16),
        vm((NZ, TILE, HID), BF16), vm((NZ, TILE, HID), BF16), vm((NZ, TILE, HID), BF16), vm((NZ, TILE, HID), BF16),
        vm((2, 4, 4, TILE, TILE), BF16), vm((2, 4, 4, TILE, TILE), BF16),
        vm((2, 4, TILE, TILE), BF16), vm((2, 4, TILE, TILE), BF16),
        vm((2, F_PAD, TILE), F32), vm((F_PAD, TILE), F32), vm((16, CHUNK, TILE), F32), vm((16, CHUNK, TILE), F32),
        vm((NZ, CHUNK, TILE), F32),
        dma, dma((4,)), dma((4,)), dma((8,)), dma((8,)), dma((4,)), dma((4,)),
        dma((8,)), dma((8,)), dma((8,)), dma((8,)), dma((2,)), dma((2,)), dma((4,)), dma((4,)),
        dma, dma, dma((8,)), dma((8,)), dma((2, 4)), dma((2, 4)), dma((2, 4)), dma((2, 4)),
        dma, dma, dma((16,)), dma((16,)), dma((8,)), dma((8,)), dma((16,)), dma((16,)), dma, dma,
    ]
    return pl.pallas_call(
        functools.partial(layer_kernel, scale),
        out_shape=(
            jax.ShapeDtypeStruct((TILE, HID), BF16),
            jax.ShapeDtypeStruct((F_IN, TILE), BF16),
            jax.ShapeDtypeStruct((16, CHUNK, HID), F32),
        ),
        in_specs=[VM] * 6,
        out_specs=(VM, VM, VM),
        scratch_shapes=scratch,
        compiler_params=pltpu.CompilerParams(
            collective_id=0, has_side_effects=True, vmem_limit_bytes=VMEM_LIMIT
        ),
    )(feat, weight, deg, cot, codes, tiles)


def per_device(node_features, weight, degree, tile_index, edge_codes, cotangent):
    scale = 1.0 / math.sqrt(node_features.shape[0] * lax.axis_size("loop"))
    out, gin, gw = layer_call(
        scale, node_features.T, weight, degree.reshape(8, TILE), cotangent, edge_codes[0], tile_index[0]
    )
    return (out, gw.reshape(F_PAD, HID)[:F_IN], gin.T)


def solution(mesh):
    return jax.shard_map(
        per_device,
        mesh=mesh,
        in_specs=(
            P("loop", None),
            P(),
            P("loop"),
            P("loop", "rep", None),
            P("loop", "rep", None, None),
            P(("loop", "rep"), None),
        ),
        out_specs=(P(("loop", "rep"), None), P(), P(("loop", "rep"), None)),
        check_vma=False,
    )
```

```python
import functools
import math

import jax
import jax.numpy as jnp
from jax import lax
from jax.experimental import pallas as pl
from jax.experimental.pallas import tpu as pltpu
from jax.sharding import PartitionSpec as P

MESH = pl.DeviceIdType.MESH
TILE = 128
HID = 256
OWN = 1024
F_IN = 602
F_PAD = 640
CHUNK = F_PAD // 16
NZ = 8
F32 = jnp.float32
BF16 = jnp.bfloat16
VM = pl.BlockSpec(memory_space=pltpu.VMEM)
VMEM_LIMIT = 56 * 1024 * 1024
Z_ORDER = (4, 3, 5, 2, 6, 1, 7)
PLANE_ORDER = (10, 9, 11, 6, 14, 2, 8, 5, 7, 13, 15, 1, 3, 4, 12)
RING_ORDER = (2, 1, 3)


def device(z, yl, k, r):
    return (z * 4 + yl * 2 + k, r)


def device_xy(z, k, x, y):
    return (z * 4 + (y % 2) * 2 + k, x * 2 + y // 2)


def remote(src, dst, send, recv, dev):
    return pltpu.make_async_remote_copy(
        src_ref=src, dst_ref=dst, send_sem=send, recv_sem=recv, device_id=dev, device_id_type=MESH
    )


def signal(sem, dev):
    pl.semaphore_signal(sem, inc=1, device_id=dev, device_id_type=MESH)


def layer_kernel(
    scale, feat_hbm, weight, deg, cot, codes, tiles,
    out, gin, gw,
    feat, pairs, relay, chunks, got, spots, slots, tbuf, dense, xall, fother, dother, ut, utw, db,
    ymate, r_y, ys, r_fwd, bt, r_one, p_part, r_two, gp, r_swap, gs, r_plane, r_z,
    feat_sem, slot_sem, code_send, code_recv, c_send, c_recv, q_send, q_recv, u_send, u_recv, v_send, v_recv, x_send, x_recv, f_send, f_recv,
    m_send, m_recv, y_send, y_recv, a_send, a_recv, b_send, b_recv,
    w_send, w_recv, g_send, g_recv, z_send, z_recv, h_send, h_recv, e_send, e_recv,
):
    l = lax.axis_index("loop")
    r = lax.axis_index("rep")
    z, yl, k = l // 4, (l // 2) % 2, l % 2
    x, yh = r // 2, r % 2
    y = yh * 2 + yl
    spot = x * 4 + y
    mate = device(z, yl, 1 - k, r)
    y_up = device_xy(z, k, x, (y + 1) % 4)
    y_down = device_xy(z, k, x, (y + 3) % 4)

    def code_source(i, rs):
        ks, yc = (k + i // 2) % 2, (yl + i % 2) % 2
        zs = (z + rs + jnp.where(2 * yl + ks - 2 * yc - k < 0, 1, 0)) % NZ
        return zs, ks, (zs == z) & (ks == k)

    def code_target(j):
        column = (l - 4 * r - j + 64) % 32
        zc, yc, kc = column // 4, (column // 2) % 2, column % 2
        slot = ((k - kc + 2) % 2) * 2 + (yc - yl + 2) % 2
        return zc, kc, slot, (zc == z) & (kc == k)

    stage = pltpu.make_async_copy(feat_hbm, feat, feat_sem)
    stage.start()
    barrier = pltpu.get_barrier_semaphore()
    signal(barrier, mate)

    def greet_z(i, carry):
        signal(barrier, device((z + i) % NZ, yl, k, r))
        return carry

    lax.fori_loop(1, NZ, greet_z, 0)

    def greet_plane(i, carry):
        signal(barrier, device_xy(z, k, (x + i // 4) % 4, (y + i) % 4))
        return carry

    lax.fori_loop(1, 16, greet_plane, 0)

    for i in range(4):
        zs, ks, mine = code_source(i, r)

        @pl.when(jnp.logical_not(mine))
        def _():
            signal(barrier, device(zs, yl, ks, r))

    kept = jnp.where(r == 0, 1 + yl, jnp.where(r == NZ - 1, 1 - yl, 0))

    for j in range(4):
        row = jnp.concatenate([tiles[j : j + 1, :], jnp.zeros((1, TILE - 32), jnp.int32)], axis=1)
        pairs[j, 0:32, :] = codes[j]
        pairs[j, 32:40, :] = jnp.broadcast_to(row, (8, TILE))

    root_rows = lax.rsqrt(deg[...].astype(F32))
    root_cols = root_rows.T
    own_root = lax.rsqrt(deg[pl.ds(r, 1), :].astype(F32))
    ut[z] = (cot[...].astype(F32).T * own_root).astype(BF16)
    stage.wait()
    for t in range(8):
        rows = slice(t * TILE, (t + 1) * TILE)
        proj = lax.dot_general(
            feat[:, rows], weight[...], (((0,), (0,)), ((), ())), preferred_element_type=F32
        )
        xall[0, rows, :] = (proj * root_cols[:, t : t + 1]).astype(BF16)

    pl.semaphore_wait(barrier, 27 - kept)

    pending = []

    def send(src, dst, s, t, dev):
        copy = remote(src, dst, s, t, dev)
        copy.start()
        pending.append(copy)
        return copy

    def code_copy(j):
        zc, kc, slot, mine = code_target(j)
        copy = remote(pairs.at[j], relay.at[slot], code_send.at[j], code_recv.at[slot], device(zc, yl, kc, r))
        return slot, mine, copy

    for j in range(4):
        slot, mine, copy = code_copy(j)

        @pl.when(mine)
        def _():
            relay[slot] = pairs[j]

        @pl.when(jnp.logical_not(mine))
        def _():
            copy.start()

    quarter = pl.ds(pl.multiple_of(512 + x * TILE, TILE), TILE)
    y_quarter = device_xy(z, k, x, (y + 1 + 2 * (x % 2)) % 4)
    f_quarter = send(feat.at[:, quarter], fother.at[:, quarter], f_send.at[3], f_recv.at[3], y_quarter)
    for i in range(4):
        zs, ks, mine = code_source(i, r)

        @pl.when(jnp.logical_not(mine))
        def _():
            remote(pairs.at[0], relay.at[i], code_send.at[i], code_recv.at[i], mate).wait_recv()

    for i in range(4):
        for t in range(8):
            chunks[t, i, 0:4, :] = relay[i, 4 * t : 4 * t + 4, :]
            chunks[t, i, 4:8, :] = relay[i, 32:36, :]
    cs = []
    for d in (3, 5, 1, 7, 2, 6, 4):
        t = (r + d) % 8
        cs.append(send(chunks.at[t], got.at[pl.ds(4 * r, 4)], c_send.at[d], c_recv.at[d], (l, t)))
    us = {
        d: send(ut.at[z], ut.at[z], u_send.at[d], u_recv.at[d], device((z + d) % NZ, yl, k, r)) for d in Z_ORDER
    }
    vs = [send(ut.at[z], ut.at[NZ + z], v_send.at[0], v_recv.at[0], mate)]
    low, high = pl.ds(0, 512), pl.ds(512, 512)
    xs = [
        send(xall.at[0, low], xall.at[1, low], x_send.at[0], x_recv.at[0], y_up),
        send(xall.at[0, high], xall.at[1, high], x_send.at[1], x_recv.at[1], y_down),
    ]
    f_low, f_high = pl.ds(0, 256), pl.ds(256, 256)
    fs = [
        send(deg, dother, f_send.at[2], f_recv.at[2], y_up),
        send(feat.at[:, f_low], fother.at[:, f_low], f_send.at[0], f_recv.at[0], y_up),
        send(feat.at[:, f_high], fother.at[:, f_high], f_send.at[1], f_recv.at[1], y_down),
    ]

    got[pl.ds(4 * r, 4)] = chunks[r]
    f_quarter.wait_recv()
    for d in RING_ORDER:
        fs.append(
            send(
                fother.at[:, quarter], fother.at[:, quarter], q_send.at[d], q_recv.at[d],
                device_xy(z, k, (x + d) % 4, y),
            )
        )
    for copy in cs:
        copy.wait_recv()

    spots[...] = got[:, 4, :]
    slot_copy = pltpu.make_async_copy(spots, slots, slot_sem)
    slot_copy.start()

    lanes = lax.broadcasted_iota(jnp.int32, (TILE, TILE), 0)

    def build(i, carry):
        block = got[i]
        for m in range(4):
            code = block[m : m + 1, :]
            rows = jnp.where(lanes == (code >> 7), 1.0, 0.0).astype(BF16)
            cols = jnp.where(lanes == (code & 127), 1.0, 0.0).astype(BF16)
            counts = lax.dot_general(rows, cols, (((1,), (1,)), ((), ())), preferred_element_type=F32)
            tbuf[i, m] = counts.astype(BF16)
        tbuf[i, 4] = jnp.zeros((TILE, TILE), BF16)
        return carry

    lax.fori_loop(0, 32, build, 0, unroll=8)
    slot_copy.wait()

    def fill(i, carry):
        zs, _, _ = code_source(i % 4, i // 4)
        w, c = ((i // 2) % 2) * NZ + zs, i % 2
        at_m = [slots[i, 4 * r + m] % 8 for m in range(4)]
        for j in range(8):
            at = jnp.int32(4)
            for m in range(4):
                at = jnp.where(at_m[m] == j, m, at)
            dense[c, pl.ds(pl.multiple_of(w * TILE, TILE), TILE), j * TILE : (j + 1) * TILE] = tbuf[i, at]
        return carry

    lax.fori_loop(0, 32, fill, 0)

    for copy in xs:
        copy.wait_recv()

    def forward(i, carry):
        rows = pl.ds(pl.multiple_of(OWN + i * 512, 512), 512)
        total = jnp.dot(dense[0, rows, :], xall[0], preferred_element_type=F32)
        total = total + jnp.dot(dense[1, rows, :], xall[1], preferred_element_type=F32)
        ymate[pl.ds(4 * i, 4)] = total.astype(BF16).reshape(4, TILE, HID)
        return carry

    lax.fori_loop(0, 2, forward, 0)
    swap_y = send(ymate, r_y, m_send, m_recv, mate)

    def forward_own(i, carry):
        rows = pl.ds(pl.multiple_of(i * 512, 512), 512)
        total = jnp.dot(dense[0, rows, :], xall[0], preferred_element_type=F32)
        total = total + jnp.dot(dense[1, rows, :], xall[1], preferred_element_type=F32)
        ys[pl.ds(4 * i, 4)] = total.astype(BF16).reshape(4, TILE, HID)
        return carry

    lax.fori_loop(0, 2, forward_own, 0)

    for d in (1, 7, 2, 6, 3, 5, 4):
        us[d].wait_recv()
        at = (z - d + NZ) % NZ
        vs.append(send(ut.at[at], ut.at[NZ + at], v_send.at[d], v_recv.at[d], mate))

    swap_y.wait_recv()
    for i in range(NZ):
        ys[i] = (ys[i].astype(F32) + r_y[i].astype(F32)).astype(BF16)
    fwd = [
        send(ys.at[(z + d) % NZ], r_fwd.at[d], y_send.at[d], y_recv.at[d], device((z + d) % NZ, yl, k, r))
        for d in Z_ORDER
    ]

    for copy in vs:
        copy.wait_recv()
    for i in range(2 * NZ):
        utw[:, i * TILE : (i + 1) * TILE] = ut[i]
    fs[0].wait_recv()
    other_rows = lax.rsqrt(dother[...].astype(F32))
    for c in range(2):
        ysd = (yl + c) % 2
        roots = root_rows if c == 0 else other_rows
        for xd in range(4):
            columns = slice(xd * 256, (xd + 1) * 256)
            prod = jnp.dot(utw[...], dense[c, :, columns], preferred_element_type=F32)
            root = jnp.concatenate([roots[2 * xd : 2 * xd + 1], roots[2 * xd + 1 : 2 * xd + 2]], axis=1)
            db[c, :, columns] = (prod * root).astype(BF16)
            prod = prod.astype(BF16)
            for h in range(2):
                piece = prod[:, h * TILE : (h + 1) * TILE]
                bt[0, xd, 2 * h + ysd] = piece[0:TILE, :]
                bt[1, 2 * h + ysd, xd] = piece[TILE:, :]

    up = (cot[...].astype(F32).T * own_root).astype(BF16).astype(F32)
    mine = pl.ds(pl.multiple_of(r * TILE, TILE), TILE)
    db[0, :, mine] = (db[0, :, mine].astype(F32) + up * own_root).astype(BF16)

    for copy in fs[1:]:
        copy.wait_recv()
    nt = (((1,), (1,)), ((), ()))
    part = lax.dot_general(feat[...], db[0], nt, preferred_element_type=F32)
    part = part + lax.dot_general(fother[...], db[1], nt, preferred_element_type=F32)
    for h in range(2):
        gp[h, 0:F_IN, :] = part[:, h * TILE : (h + 1) * TILE]
        gp[h, F_IN:F_PAD, :] = jnp.zeros((F_PAD - F_IN, TILE), F32)
    swap = send(gp.at[1 - k], r_swap, w_send, w_recv, mate)
    swap.wait_recv()
    gs[...] = (gp[k] + r_swap[...]).reshape(16, CHUNK, TILE)

    planes = []
    for i in PLANE_ORDER:
        xd, yd = (x + i // 4) % 4, (y + i % 4) % 4
        planes.append(
            send(gs.at[xd * 4 + yd], r_plane.at[i], g_send.at[i], g_recv.at[i], device_xy(z, k, xd, yd))
        )

    here = (x, y)
    ones = []
    for d in RING_ORDER:
        for h in range(2):
            at = (here[h] + d) % 4
            dev = device_xy(z, k, (x + d) % 4, y) if h == 0 else device_xy(z, k, x, (y + d) % 4)
            ones.append(send(bt.at[h, at], r_one.at[h, d], a_send.at[h, d], a_recv.at[h, d], dev))

    for copy in planes:
        copy.wait_recv()
    total = gs[spot]
    for i in range(1, 16):
        total = total + r_plane[i]
    r_z[z] = total
    zs = [
        send(r_z.at[z], r_z.at[z], z_send.at[d], z_recv.at[d], device((z + d) % NZ, yl, k, r)) for d in Z_ORDER
    ]

    for copy in ones:
        copy.wait_recv()
    twos = []
    for d in RING_ORDER + (0,):
        for h in range(2):
            at = (here[1 - h] + d) % 4
            total = bt[h, here[h], at].astype(F32)
            for e in range(1, 4):
                total = total + r_one[h, e, at].astype(F32)
            if d:
                p_part[h, d] = total.astype(BF16)
                dev = device_xy(z, k, x, (y + d) % 4) if h == 0 else device_xy(z, k, (x + d) % 4, y)
                twos.append(send(p_part.at[h, d], r_two.at[h, d], b_send.at[h, d], b_recv.at[h, d], dev))
            elif h == 0:
                top = total
            else:
                bottom = total

    for copy in zs:
        copy.wait_recv()
    total = r_z[0]
    for i in range(1, NZ):
        total = total + r_z[i]
    half = pl.ds(pl.multiple_of(k * TILE, TILE), TILE)
    gw[spot, :, half] = total * scale
    spread = []
    for i in PLANE_ORDER:
        xd, yd = (x + i // 4) % 4, (y + i % 4) % 4
        spread.append(
            send(gw.at[spot, :, half], gw.at[spot, :, half], h_send.at[i], h_recv.at[i], device_xy(z, k, xd, yd))
        )

    for copy in twos:
        copy.wait_recv()
    for e in range(1, 4):
        top = top + r_two[0, e].astype(F32)
        bottom = bottom + r_two[1, e].astype(F32)
    back = jnp.concatenate([top, bottom], axis=0) + up
    node_grad = (back * own_root).astype(BF16)
    gin[...] = jnp.dot(weight[...], node_grad, preferred_element_type=F32).astype(BF16)

    for copy in fwd:
        copy.wait_recv()
    total = ys[z].astype(F32) + xall[0, mine, :].astype(F32)
    for d in range(1, NZ):
        total = total + r_fwd[d].astype(F32)
    root_col = jnp.broadcast_to(own_root, (8, TILE)).T
    out[...] = (total * root_col[:, 0:1]).astype(BF16)

    for copy in spread:
        copy.wait_recv()
    last = send(gw.at[:, :, half], gw.at[:, :, half], e_send, e_recv, mate)

    for j in range(4):
        _, mine, copy = code_copy(j)

        @pl.when(jnp.logical_not(mine))
        def _():
            copy.wait_send()

    last.wait_recv()
    for copy in pending:
        copy.wait_send()


def layer_call(scale, feat, weight, deg, cot, codes, tiles):
    dma = pltpu.SemaphoreType.DMA
    vm = pltpu.VMEM
    i32 = jnp.int32
    scratch = [
        vm((F_IN, OWN), BF16), vm((4, 40, TILE), i32), vm((4, 40, TILE), i32), vm((8, 4, 8, TILE), i32), vm((32, 8, TILE), i32), vm((32, TILE), i32), pltpu.SMEM((32, TILE), i32),
        vm((32, 5, TILE, TILE), BF16), vm((2, 2 * OWN, OWN), BF16), vm((2, OWN, HID), BF16),
        vm((F_IN, OWN), BF16), vm((8, TILE), i32), vm((2 * NZ, HID, TILE), BF16),
        vm((HID, 2 * OWN), BF16), vm((2, HID, OWN), BF16),
        vm((NZ, TILE, HID), BF16), vm((NZ, TILE, HID), BF16), vm((NZ, TILE, HID), BF16), vm((NZ, TILE, HID), BF16),
        vm((2, 4, 4, TILE, TILE), BF16), vm((2, 4, 4, TILE, TILE), BF16),
        vm((2, 4, TILE, TILE), BF16), vm((2, 4, TILE, TILE), BF16),
        vm((2, F_PAD, TILE), F32), vm((F_PAD, TILE), F32), vm((16, CHUNK, TILE), F32), vm((16, CHUNK, TILE), F32),
        vm((NZ, CHUNK, TILE), F32),
        dma, dma, dma((4,)), dma((4,)), dma((8,)), dma((8,)), dma((4,)), dma((4,)),
        dma((8,)), dma((8,)), dma((8,)), dma((8,)), dma((2,)), dma((2,)), dma((4,)), dma((4,)),
        dma, dma, dma((8,)), dma((8,)), dma((2, 4)), dma((2, 4)), dma((2, 4)), dma((2, 4)),
        dma, dma, dma((16,)), dma((16,)), dma((8,)), dma((8,)), dma((16,)), dma((16,)), dma, dma,
    ]
    return pl.pallas_call(
        functools.partial(layer_kernel, scale),
        out_shape=(
            jax.ShapeDtypeStruct((TILE, HID), BF16),
            jax.ShapeDtypeStruct((F_IN, TILE), BF16),
            jax.ShapeDtypeStruct((16, CHUNK, HID), F32),
        ),
        in_specs=[pl.BlockSpec(memory_space=pl.ANY)] + [VM] * 5,
        out_specs=(VM, VM, VM),
        scratch_shapes=scratch,
        compiler_params=pltpu.CompilerParams(
            collective_id=0, has_side_effects=True, vmem_limit_bytes=VMEM_LIMIT
        ),
    )(feat, weight, deg, cot, codes, tiles)


def per_device(node_features, weight, degree, tile_index, edge_codes, cotangent):
    scale = 1.0 / math.sqrt(node_features.shape[0] * lax.axis_size("loop"))
    out, gin, gw = layer_call(
        scale, node_features.T, weight, degree.reshape(8, TILE), cotangent, edge_codes[0], tile_index[0]
    )
    return (out, gw.reshape(F_PAD, HID)[:F_IN], gin.T)


def solution(mesh):
    return jax.shard_map(
        per_device,
        mesh=mesh,
        in_specs=(
            P("loop", None),
            P(),
            P("loop"),
            P("loop", "rep", None),
            P("loop", "rep", None, None),
            P(("loop", "rep"), None),
        ),
        out_specs=(P(("loop", "rep"), None), P(), P(("loop", "rep"), None)),
        check_vma=False,
    )
```

```python
import functools
import math

import jax
import jax.numpy as jnp
from jax import lax
from jax.experimental import pallas as pl
from jax.experimental.pallas import tpu as pltpu
from jax.sharding import PartitionSpec as P

MESH = pl.DeviceIdType.MESH
TILE = 128
HID = 256
OWN = 1024
F_IN = 602
F_PAD = 640
CHUNK = F_PAD // 16
WIRE = 48
NZ = 8
F32 = jnp.float32
BF16 = jnp.bfloat16
VM = pl.BlockSpec(memory_space=pltpu.VMEM)
VMEM_LIMIT = 56 * 1024 * 1024
Z_ORDER = (4, 3, 5, 2, 6, 1, 7)
PLANE_ORDER = (10, 9, 11, 6, 14, 2, 8, 5, 7, 13, 15, 1, 3, 4, 12)
RING_ORDER = (2, 1, 3)


def device(z, yl, k, r):
    return (z * 4 + yl * 2 + k, r)


def device_xy(z, k, x, y):
    return (z * 4 + (y % 2) * 2 + k, x * 2 + y // 2)


def remote(src, dst, send, recv, dev):
    return pltpu.make_async_remote_copy(
        src_ref=src, dst_ref=dst, send_sem=send, recv_sem=recv, device_id=dev, device_id_type=MESH
    )


def signal(sem, dev):
    pl.semaphore_signal(sem, inc=1, device_id=dev, device_id_type=MESH)


def layer_kernel(
    scale, feat_hbm, weight, deg, cot, codes, tiles,
    out, gin, gw,
    gsend, feat, pairs, relay, chunks, got, spots, slots, tbuf, dense, xall, fother, dother, ut, utw, db,
    ymate, r_y, ys, r_fwd, bt, r_one, p_part, r_two, gp, r_swap, gs, r_plane, r_z,
    feat_sem, slot_sem, code_send, code_recv, c_send, c_recv, q_send, q_recv, u_send, u_recv, v_send, v_recv, x_send, x_recv, f_send, f_recv,
    m_send, m_recv, y_send, y_recv, a_send, a_recv, b_send, b_recv,
    w_send, w_recv, g_send, g_recv, z_send, z_recv, h_send, h_recv, e_send, e_recv,
):
    l = lax.axis_index("loop")
    r = lax.axis_index("rep")
    z, yl, k = l // 4, (l // 2) % 2, l % 2
    x, yh = r // 2, r % 2
    y = yh * 2 + yl
    spot = x * 4 + y
    mate = device(z, yl, 1 - k, r)
    y_up = device_xy(z, k, x, (y + 1) % 4)
    y_down = device_xy(z, k, x, (y + 3) % 4)

    def code_source(i, rs):
        ks, yc = (k + i // 2) % 2, (yl + i % 2) % 2
        zs = (z + rs + jnp.where(2 * yl + ks - 2 * yc - k < 0, 1, 0)) % NZ
        return zs, ks, (zs == z) & (ks == k)

    def code_target(j):
        column = (l - 4 * r - j + 64) % 32
        zc, yc, kc = column // 4, (column // 2) % 2, column % 2
        slot = ((k - kc + 2) % 2) * 2 + (yc - yl + 2) % 2
        return zc, kc, slot, (zc == z) & (kc == k)

    stage = pltpu.make_async_copy(feat_hbm, feat, feat_sem)
    stage.start()
    barrier = pltpu.get_barrier_semaphore()
    signal(barrier, mate)

    def greet_z(i, carry):
        signal(barrier, device((z + i) % NZ, yl, k, r))
        return carry

    lax.fori_loop(1, NZ, greet_z, 0)

    def greet_plane(i, carry):
        signal(barrier, device_xy(z, k, (x + i // 4) % 4, (y + i) % 4))
        return carry

    lax.fori_loop(1, 16, greet_plane, 0)

    for i in range(4):
        zs, ks, mine = code_source(i, r)

        @pl.when(jnp.logical_not(mine))
        def _():
            signal(barrier, device(zs, yl, ks, r))

    kept = jnp.where(r == 0, 1 + yl, jnp.where(r == NZ - 1, 1 - yl, 0))

    for j in range(4):
        row = jnp.concatenate([tiles[j : j + 1, :], jnp.zeros((1, TILE - 32), jnp.int32)], axis=1)
        pairs[j, 0:32, :] = codes[j]
        pairs[j, 32:40, :] = jnp.broadcast_to(row, (8, TILE))

    root_rows = lax.rsqrt(deg[...].astype(F32))
    root_cols = root_rows.T
    own_root = lax.rsqrt(deg[pl.ds(r, 1), :].astype(F32))
    ut[z] = (cot[...].astype(F32).T * own_root).astype(BF16)
    stage.wait()
    for t in range(8):
        rows = slice(t * TILE, (t + 1) * TILE)
        proj = lax.dot_general(
            feat[:, rows], weight[...], (((0,), (0,)), ((), ())), preferred_element_type=F32
        )
        xall[0, rows, :] = (proj * root_cols[:, t : t + 1]).astype(BF16)

    pl.semaphore_wait(barrier, 27 - kept)

    pending = []

    def send(src, dst, s, t, dev):
        copy = remote(src, dst, s, t, dev)
        copy.start()
        pending.append(copy)
        return copy

    def code_copy(j):
        zc, kc, slot, mine = code_target(j)
        copy = remote(pairs.at[j], relay.at[slot], code_send.at[j], code_recv.at[slot], device(zc, yl, kc, r))
        return slot, mine, copy

    for j in range(4):
        slot, mine, copy = code_copy(j)

        @pl.when(mine)
        def _():
            relay[slot] = pairs[j]

        @pl.when(jnp.logical_not(mine))
        def _():
            copy.start()

    quarter = pl.ds(pl.multiple_of(512 + x * TILE, TILE), TILE)
    y_quarter = device_xy(z, k, x, (y + 1 + 2 * (x % 2)) % 4)
    f_quarter = send(feat.at[:, quarter], fother.at[:, quarter], f_send.at[3], f_recv.at[3], y_quarter)
    for i in range(4):
        zs, ks, mine = code_source(i, r)

        @pl.when(jnp.logical_not(mine))
        def _():
            remote(pairs.at[0], relay.at[i], code_send.at[i], code_recv.at[i], mate).wait_recv()

    for i in range(4):
        for t in range(8):
            chunks[t, i, 0:4, :] = relay[i, 4 * t : 4 * t + 4, :]
            chunks[t, i, 4:8, :] = relay[i, 32:36, :]
    cs = []
    for d in (3, 5, 1, 7, 2, 6, 4):
        t = (r + d) % 8
        cs.append(send(chunks.at[t], got.at[pl.ds(4 * r, 4)], c_send.at[d], c_recv.at[d], (l, t)))
    us = {
        d: send(ut.at[z], ut.at[z], u_send.at[d], u_recv.at[d], device((z + d) % NZ, yl, k, r)) for d in Z_ORDER
    }
    vs = [send(ut.at[z], ut.at[NZ + z], v_send.at[0], v_recv.at[0], mate)]
    low, high = pl.ds(0, 512), pl.ds(512, 512)
    xs = [
        send(xall.at[0, low], xall.at[1, low], x_send.at[0], x_recv.at[0], y_up),
        send(xall.at[0, high], xall.at[1, high], x_send.at[1], x_recv.at[1], y_down),
    ]
    f_low, f_high = pl.ds(0, 256), pl.ds(256, 256)
    fs = [
        send(deg, dother, f_send.at[2], f_recv.at[2], y_up),
        send(feat.at[:, f_low], fother.at[:, f_low], f_send.at[0], f_recv.at[0], y_up),
        send(feat.at[:, f_high], fother.at[:, f_high], f_send.at[1], f_recv.at[1], y_down),
    ]

    got[pl.ds(4 * r, 4)] = chunks[r]
    f_quarter.wait_recv()
    for d in RING_ORDER:
        fs.append(
            send(
                fother.at[:, quarter], fother.at[:, quarter], q_send.at[d], q_recv.at[d],
                device_xy(z, k, (x + d) % 4, y),
            )
        )
    lanes = lax.broadcasted_iota(jnp.int32, (TILE, TILE), 0)

    def group(rs):
        block = got[pl.ds(4 * rs, 4)]
        where = block[:, 4, :]
        spots[rs] = jnp.concatenate([where, where], axis=0)
        slot_copy = pltpu.make_async_copy(spots.at[rs], slots.at[rs], slot_sem.at[rs])
        slot_copy.start()
        for i in range(4):
            for m in range(4):
                code = block[i, m : m + 1, :]
                rows = jnp.where(lanes == (code >> 7), 1.0, 0.0).astype(BF16)
                cols = jnp.where(lanes == (code & 127), 1.0, 0.0).astype(BF16)
                counts = lax.dot_general(rows, cols, (((1,), (1,)), ((), ())), preferred_element_type=F32)
                tbuf[i, m] = counts.astype(BF16)
            tbuf[i, 4] = jnp.zeros((TILE, TILE), BF16)
        slot_copy.wait()
        for i in range(4):
            zs, _, _ = code_source(i, rs)
            w, c = (i // 2) * NZ + zs, i % 2
            at_m = [slots[rs, i, 4 * r + m] % 8 for m in range(4)]
            for j in range(8):
                at = jnp.int32(4)
                for m in range(4):
                    at = jnp.where(at_m[m] == j, m, at)
                dense[c, pl.ds(pl.multiple_of(w * TILE, TILE), TILE), j * TILE : (j + 1) * TILE] = tbuf[i, at]

    group(r)

    def arrived(n, carry):
        d = jnp.where(n < 4, 2 * n, 2 * n - 7)
        rs = (r - d + 8) % 8
        remote(chunks.at[0], got.at[pl.ds(4 * rs, 4)], c_send.at[d], c_recv.at[d], mate).wait_recv()
        group(rs)
        return carry

    lax.fori_loop(1, 8, arrived, 0)

    for copy in xs:
        copy.wait_recv()

    def forward(i, carry):
        rows = pl.ds(pl.multiple_of(OWN + i * 512, 512), 512)
        total = jnp.dot(dense[0, rows, :], xall[0], preferred_element_type=F32)
        total = total + jnp.dot(dense[1, rows, :], xall[1], preferred_element_type=F32)
        ymate[pl.ds(4 * i, 4)] = total.astype(BF16).reshape(4, TILE, HID)
        return carry

    lax.fori_loop(0, 2, forward, 0)
    swap_y = send(ymate, r_y, m_send, m_recv, mate)

    def forward_own(i, carry):
        rows = pl.ds(pl.multiple_of(i * 512, 512), 512)
        total = jnp.dot(dense[0, rows, :], xall[0], preferred_element_type=F32)
        total = total + jnp.dot(dense[1, rows, :], xall[1], preferred_element_type=F32)
        ys[pl.ds(4 * i, 4)] = total.astype(BF16).reshape(4, TILE, HID)
        return carry

    lax.fori_loop(0, 2, forward_own, 0)

    for d in (1, 7, 2, 6, 3, 5, 4):
        us[d].wait_recv()
        at = (z - d + NZ) % NZ
        vs.append(send(ut.at[at], ut.at[NZ + at], v_send.at[d], v_recv.at[d], mate))

    swap_y.wait_recv()
    for i in range(NZ):
        ys[i] = (ys[i].astype(F32) + r_y[i].astype(F32)).astype(BF16)
    fwd = [
        send(ys.at[(z + d) % NZ], r_fwd.at[d], y_send.at[d], y_recv.at[d], device((z + d) % NZ, yl, k, r))
        for d in Z_ORDER
    ]

    for copy in vs:
        copy.wait_recv()
    for i in range(2 * NZ):
        utw[:, i * TILE : (i + 1) * TILE] = ut[i]
    fs[0].wait_recv()
    other_rows = lax.rsqrt(dother[...].astype(F32))
    for c in range(2):
        ysd = (yl + c) % 2
        roots = root_rows if c == 0 else other_rows
        for xd in range(4):
            columns = slice(xd * 256, (xd + 1) * 256)
            prod = jnp.dot(utw[...], dense[c, :, columns], preferred_element_type=F32)
            root = jnp.concatenate([roots[2 * xd : 2 * xd + 1], roots[2 * xd + 1 : 2 * xd + 2]], axis=1)
            db[c, :, columns] = (prod * root).astype(BF16)
            prod = prod.astype(BF16)
            for h in range(2):
                piece = prod[:, h * TILE : (h + 1) * TILE]
                bt[0, xd, 2 * h + ysd] = piece[0:TILE, :]
                bt[1, 2 * h + ysd, xd] = piece[TILE:, :]

    up = (cot[...].astype(F32).T * own_root).astype(BF16).astype(F32)
    mine = pl.ds(pl.multiple_of(r * TILE, TILE), TILE)
    db[0, :, mine] = (db[0, :, mine].astype(F32) + up * own_root).astype(BF16)

    for copy in fs[1:]:
        copy.wait_recv()
    nt = (((1,), (1,)), ((), ()))
    part = lax.dot_general(feat[...], db[0], nt, preferred_element_type=F32)
    part = part + lax.dot_general(fother[...], db[1], nt, preferred_element_type=F32)
    for h in range(2):
        gp[h, 0:F_IN, :] = part[:, h * TILE : (h + 1) * TILE]
        gp[h, F_IN:F_PAD, :] = jnp.zeros((F_PAD - F_IN, TILE), F32)
    swap = send(gp.at[1 - k], r_swap, w_send, w_recv, mate)
    swap.wait_recv()
    gs[...] = (gp[k] + r_swap[...]).reshape(16, CHUNK, TILE)
    gsend[:, 0:CHUNK, :] = gs[...].astype(BF16)
    gsend[:, CHUNK:WIRE, :] = jnp.zeros((16, WIRE - CHUNK, TILE), BF16)

    planes = []
    for i in PLANE_ORDER:
        xd, yd = (x + i // 4) % 4, (y + i % 4) % 4
        planes.append(
            send(gsend.at[xd * 4 + yd], r_plane.at[i], g_send.at[i], g_recv.at[i], device_xy(z, k, xd, yd))
        )

    here = (x, y)
    ones = []
    for d in RING_ORDER:
        for h in range(2):
            at = (here[h] + d) % 4
            dev = device_xy(z, k, (x + d) % 4, y) if h == 0 else device_xy(z, k, x, (y + d) % 4)
            ones.append(send(bt.at[h, at], r_one.at[h, d], a_send.at[h, d], a_recv.at[h, d], dev))

    for copy in planes:
        copy.wait_recv()
    total = gs[spot]
    for i in range(1, 16):
        total = total + r_plane[i, 0:CHUNK, :].astype(F32)
    r_z[z] = jnp.concatenate([total, jnp.zeros((WIRE - CHUNK, TILE), F32)], axis=0).astype(BF16)
    zs = [
        send(r_z.at[z], r_z.at[z], z_send.at[d], z_recv.at[d], device((z + d) % NZ, yl, k, r)) for d in Z_ORDER
    ]

    for copy in ones:
        copy.wait_recv()
    twos = []
    for d in RING_ORDER + (0,):
        for h in range(2):
            at = (here[1 - h] + d) % 4
            total = bt[h, here[h], at].astype(F32)
            for e in range(1, 4):
                total = total + r_one[h, e, at].astype(F32)
            if d:
                p_part[h, d] = total.astype(BF16)
                dev = device_xy(z, k, x, (y + d) % 4) if h == 0 else device_xy(z, k, (x + d) % 4, y)
                twos.append(send(p_part.at[h, d], r_two.at[h, d], b_send.at[h, d], b_recv.at[h, d], dev))
            elif h == 0:
                top = total
            else:
                bottom = total

    for copy in zs:
        copy.wait_recv()
    total = r_z[0, 0:CHUNK, :].astype(F32)
    for i in range(1, NZ):
        total = total + r_z[i, 0:CHUNK, :].astype(F32)
    half = pl.ds(pl.multiple_of(k * TILE, TILE), TILE)
    gw[spot, :, half] = total * scale
    spread = []
    for i in PLANE_ORDER:
        xd, yd = (x + i // 4) % 4, (y + i % 4) % 4
        spread.append(
            send(gw.at[spot, :, half], gw.at[spot, :, half], h_send.at[i], h_recv.at[i], device_xy(z, k, xd, yd))
        )

    for copy in twos:
        copy.wait_recv()
    for e in range(1, 4):
        top = top + r_two[0, e].astype(F32)
        bottom = bottom + r_two[1, e].astype(F32)
    back = jnp.concatenate([top, bottom], axis=0) + up
    node_grad = (back * own_root).astype(BF16)
    gin[...] = jnp.dot(weight[...], node_grad, preferred_element_type=F32).astype(BF16)

    for copy in fwd:
        copy.wait_recv()
    total = ys[z].astype(F32) + xall[0, mine, :].astype(F32)
    for d in range(1, NZ):
        total = total + r_fwd[d].astype(F32)
    root_col = jnp.broadcast_to(own_root, (8, TILE)).T
    out[...] = (total * root_col[:, 0:1]).astype(BF16)

    for copy in spread:
        copy.wait_recv()
    last = send(gw.at[:, :, half], gw.at[:, :, half], e_send, e_recv, mate)

    for j in range(4):
        _, mine, copy = code_copy(j)

        @pl.when(jnp.logical_not(mine))
        def _():
            copy.wait_send()

    last.wait_recv()
    for copy in pending:
        copy.wait_send()


def layer_call(scale, feat, weight, deg, cot, codes, tiles):
    dma = pltpu.SemaphoreType.DMA
    vm = pltpu.VMEM
    i32 = jnp.int32
    scratch = [
        vm((16, WIRE, TILE), BF16), vm((F_IN, OWN), BF16), vm((4, 40, TILE), i32), vm((4, 40, TILE), i32), vm((8, 4, 8, TILE), i32), vm((32, 8, TILE), i32), vm((8, 8, TILE), i32), pltpu.SMEM((8, 8, TILE), i32),
        vm((4, 5, TILE, TILE), BF16), vm((2, 2 * OWN, OWN), BF16), vm((2, OWN, HID), BF16),
        vm((F_IN, OWN), BF16), vm((8, TILE), i32), vm((2 * NZ, HID, TILE), BF16),
        vm((HID, 2 * OWN), BF16), vm((2, HID, OWN), BF16),
        vm((NZ, TILE, HID), BF16), vm((NZ, TILE, HID), BF16), vm((NZ, TILE, HID), BF16), vm((NZ, TILE, HID), BF16),
        vm((2, 4, 4, TILE, TILE), BF16), vm((2, 4, 4, TILE, TILE), BF16),
        vm((2, 4, TILE, TILE), BF16), vm((2, 4, TILE, TILE), BF16),
        vm((2, F_PAD, TILE), F32), vm((F_PAD, TILE), F32), vm((16, CHUNK, TILE), F32), vm((16, WIRE, TILE), BF16),
        vm((NZ, WIRE, TILE), BF16),
        dma, dma((8,)), dma((4,)), dma((4,)), dma((8,)), dma((8,)), dma((4,)), dma((4,)),
        dma((8,)), dma((8,)), dma((8,)), dma((8,)), dma((2,)), dma((2,)), dma((4,)), dma((4,)),
        dma, dma, dma((8,)), dma((8,)), dma((2, 4)), dma((2, 4)), dma((2, 4)), dma((2, 4)),
        dma, dma, dma((16,)), dma((16,)), dma((8,)), dma((8,)), dma((16,)), dma((16,)), dma, dma,
    ]
    return pl.pallas_call(
        functools.partial(layer_kernel, scale),
        out_shape=(
            jax.ShapeDtypeStruct((TILE, HID), BF16),
            jax.ShapeDtypeStruct((F_IN, TILE), BF16),
            jax.ShapeDtypeStruct((16, CHUNK, HID), F32),
        ),
        in_specs=[pl.BlockSpec(memory_space=pl.ANY)] + [VM] * 5,
        out_specs=(VM, VM, VM),
        scratch_shapes=scratch,
        compiler_params=pltpu.CompilerParams(
            collective_id=0, has_side_effects=True, vmem_limit_bytes=VMEM_LIMIT
        ),
    )(feat, weight, deg, cot, codes, tiles)


def per_device(node_features, weight, degree, tile_index, edge_codes, cotangent):
    scale = 1.0 / math.sqrt(node_features.shape[0] * lax.axis_size("loop"))
    out, gin, gw = layer_call(
        scale, node_features.T, weight, degree.reshape(8, TILE), cotangent, edge_codes[0], tile_index[0]
    )
    return (out, gw.reshape(F_PAD, HID)[:F_IN], gin.T)


def solution(mesh):
    return jax.shard_map(
        per_device,
        mesh=mesh,
        in_specs=(
            P("loop", None),
            P(),
            P("loop"),
            P("loop", "rep", None),
            P("loop", "rep", None, None),
            P(("loop", "rep"), None),
        ),
        out_specs=(P(("loop", "rep"), None), P(), P(("loop", "rep"), None)),
        check_vma=False,
    )
```

```python
import functools
import math

import jax
import jax.numpy as jnp
from jax import lax
from jax.experimental import pallas as pl
from jax.experimental.pallas import tpu as pltpu
from jax.sharding import PartitionSpec as P

MESH = pl.DeviceIdType.MESH
TILE = 128
HID = 256
OWN = 1024
F_IN = 602
F_PAD = 640
CHUNK = F_PAD // 16
WIRE = 48
NZ = 8
F32 = jnp.float32
BF16 = jnp.bfloat16
VM = pl.BlockSpec(memory_space=pltpu.VMEM)
VMEM_LIMIT = 56 * 1024 * 1024
Z_ORDER = (4, 3, 5, 2, 6, 1, 7)
PLANE_ORDER = (10, 9, 11, 6, 14, 2, 8, 5, 7, 13, 15, 1, 3, 4, 12)
RING_ORDER = (2, 1, 3)


def device(z, yl, k, r):
    return (z * 4 + yl * 2 + k, r)


def device_xy(z, k, x, y):
    return (z * 4 + (y % 2) * 2 + k, x * 2 + y // 2)


def remote(src, dst, send, recv, dev):
    return pltpu.make_async_remote_copy(
        src_ref=src, dst_ref=dst, send_sem=send, recv_sem=recv, device_id=dev, device_id_type=MESH
    )


def signal(sem, dev):
    pl.semaphore_signal(sem, inc=1, device_id=dev, device_id_type=MESH)


def layer_kernel(
    scale, feat_hbm, weight, deg, cot, codes, tiles,
    out, gin, gw,
    gsend, feat, pairs, relay, chunks, got, spots, slots, tbuf, dense, xall, fother, dother, ut, utw, db,
    ymate, r_y, ys, r_fwd, bt, r_one, p_part, r_two, gp, r_swap, gs, r_plane, r_z,
    feat_sem, slot_sem, code_send, code_recv, c_send, c_recv, q_send, q_recv, u_send, u_recv, v_send, v_recv, x_send, x_recv, f_send, f_recv,
    m_send, m_recv, y_send, y_recv, a_send, a_recv, b_send, b_recv,
    w_send, w_recv, g_send, g_recv, z_send, z_recv, h_send, h_recv, e_send, e_recv,
):
    l = lax.axis_index("loop")
    r = lax.axis_index("rep")
    z, yl, k = l // 4, (l // 2) % 2, l % 2
    x, yh = r // 2, r % 2
    y = yh * 2 + yl
    spot = x * 4 + y
    mate = device(z, yl, 1 - k, r)
    y_up = device_xy(z, k, x, (y + 1) % 4)
    y_down = device_xy(z, k, x, (y + 3) % 4)

    def code_source(i, rs):
        ks, yc = (k + i // 2) % 2, (yl + i % 2) % 2
        zs = (z + rs + jnp.where(2 * yl + ks - 2 * yc - k < 0, 1, 0)) % NZ
        return zs, ks, (zs == z) & (ks == k)

    def code_target(j):
        column = (l - 4 * r - j + 64) % 32
        zc, yc, kc = column // 4, (column // 2) % 2, column % 2
        slot = ((k - kc + 2) % 2) * 2 + (yc - yl + 2) % 2
        return zc, kc, slot, (zc == z) & (kc == k)

    stage = pltpu.make_async_copy(feat_hbm, feat, feat_sem)
    stage.start()
    barrier = pltpu.get_barrier_semaphore()
    signal(barrier, mate)

    def greet_z(i, carry):
        signal(barrier, device((z + i) % NZ, yl, k, r))
        return carry

    lax.fori_loop(1, NZ, greet_z, 0)

    def greet_plane(i, carry):
        signal(barrier, device_xy(z, k, (x + i // 4) % 4, (y + i) % 4))
        return carry

    lax.fori_loop(1, 16, greet_plane, 0)

    for i in range(4):
        zs, ks, mine = code_source(i, r)

        @pl.when(jnp.logical_not(mine))
        def _():
            signal(barrier, device(zs, yl, ks, r))

    kept = jnp.where(r == 0, 1 + yl, jnp.where(r == NZ - 1, 1 - yl, 0))

    for j in range(4):
        row = jnp.concatenate([tiles[j : j + 1, :], jnp.zeros((1, TILE - 32), jnp.int32)], axis=1)
        pairs[j, 0:32, :] = codes[j]
        pairs[j, 32:40, :] = jnp.broadcast_to(row, (8, TILE))

    root_rows = lax.rsqrt(deg[...].astype(F32))
    root_cols = root_rows.T
    own_root = lax.rsqrt(deg[pl.ds(r, 1), :].astype(F32))
    ut[z] = (cot[...].astype(F32).T * own_root).astype(BF16)
    stage.wait()
    for t in range(8):
        rows = slice(t * TILE, (t + 1) * TILE)
        proj = lax.dot_general(
            feat[:, rows], weight[...], (((0,), (0,)), ((), ())), preferred_element_type=F32
        )
        xall[0, rows, :] = (proj * root_cols[:, t : t + 1]).astype(BF16)

    pl.semaphore_wait(barrier, 27 - kept)

    pending = []

    def send(src, dst, s, t, dev):
        copy = remote(src, dst, s, t, dev)
        copy.start()
        pending.append(copy)
        return copy

    def code_copy(j):
        zc, kc, slot, mine = code_target(j)
        copy = remote(pairs.at[j], relay.at[slot], code_send.at[j], code_recv.at[slot], device(zc, yl, kc, r))
        return slot, mine, copy

    for j in range(4):
        slot, mine, copy = code_copy(j)

        @pl.when(mine)
        def _():
            relay[slot] = pairs[j]

        @pl.when(jnp.logical_not(mine))
        def _():
            copy.start()

    quarter = pl.ds(pl.multiple_of(512 + x * TILE, TILE), TILE)
    y_quarter = device_xy(z, k, x, (y + 1 + 2 * (x % 2)) % 4)
    f_quarter = send(feat.at[:, quarter], fother.at[:, quarter], f_send.at[3], f_recv.at[3], y_quarter)
    for i in range(4):
        zs, ks, mine = code_source(i, r)

        @pl.when(jnp.logical_not(mine))
        def _():
            remote(pairs.at[0], relay.at[i], code_send.at[i], code_recv.at[i], mate).wait_recv()

    for i in range(4):
        for t in range(8):
            chunks[t, i, 0:4, :] = relay[i, 4 * t : 4 * t + 4, :]
            chunks[t, i, 4:8, :] = relay[i, 32:36, :]
    cs = []
    for d in (3, 5, 1, 7, 2, 6, 4):
        t = (r + d) % 8
        cs.append(send(chunks.at[t], got.at[pl.ds(4 * r, 4)], c_send.at[d], c_recv.at[d], (l, t)))
    us = {
        d: send(ut.at[z], ut.at[z], u_send.at[d], u_recv.at[d], device((z + d) % NZ, yl, k, r)) for d in Z_ORDER
    }
    vs = [send(ut.at[z], ut.at[NZ + z], v_send.at[0], v_recv.at[0], mate)]
    low, high = pl.ds(0, 512), pl.ds(512, 512)
    xs = [
        send(xall.at[0, low], xall.at[1, low], x_send.at[0], x_recv.at[0], y_up),
        send(xall.at[0, high], xall.at[1, high], x_send.at[1], x_recv.at[1], y_down),
    ]
    f_low, f_high = pl.ds(0, 256), pl.ds(256, 256)
    fs = [
        send(deg, dother, f_send.at[2], f_recv.at[2], y_up),
        send(feat.at[:, f_low], fother.at[:, f_low], f_send.at[0], f_recv.at[0], y_up),
        send(feat.at[:, f_high], fother.at[:, f_high], f_send.at[1], f_recv.at[1], y_down),
    ]

    got[pl.ds(4 * r, 4)] = chunks[r]
    f_quarter.wait_recv()
    for d in RING_ORDER:
        fs.append(
            send(
                fother.at[:, quarter], fother.at[:, quarter], q_send.at[d], q_recv.at[d],
                device_xy(z, k, (x + d) % 4, y),
            )
        )
    lanes = lax.broadcasted_iota(jnp.int32, (TILE, TILE), 0)

    def group(rs):
        block = got[pl.ds(4 * rs, 4)]
        where = block[:, 4, :]
        spots[rs] = jnp.concatenate([where, where], axis=0)
        slot_copy = pltpu.make_async_copy(spots.at[rs], slots.at[rs], slot_sem.at[rs])
        slot_copy.start()
        for i in range(4):
            for m in range(4):
                code = block[i, m : m + 1, :]
                rows = jnp.where(lanes == (code >> 7), 1.0, 0.0).astype(BF16)
                cols = jnp.where(lanes == (code & 127), 1.0, 0.0).astype(BF16)
                counts = lax.dot_general(rows, cols, (((1,), (1,)), ((), ())), preferred_element_type=F32)
                tbuf[i, m] = counts.astype(BF16)
            tbuf[i, 4] = jnp.zeros((TILE, TILE), BF16)
        slot_copy.wait()
        for i in range(4):
            zs, _, _ = code_source(i, rs)
            w, c = (i // 2) * NZ + zs, i % 2
            at_m = [slots[rs, i, 4 * r + m] % 8 for m in range(4)]
            for j in range(8):
                at = jnp.int32(4)
                for m in range(4):
                    at = jnp.where(at_m[m] == j, m, at)
                dense[c, pl.ds(pl.multiple_of(w * TILE, TILE), TILE), j * TILE : (j + 1) * TILE] = tbuf[i, at]

    group(r)

    def arrived(n, carry):
        d = jnp.where(n < 4, 2 * n, 2 * n - 7)
        rs = (r - d + 8) % 8
        remote(chunks.at[0], got.at[pl.ds(4 * rs, 4)], c_send.at[d], c_recv.at[d], mate).wait_recv()
        group(rs)
        return carry

    lax.fori_loop(1, 8, arrived, 0)

    for copy in xs:
        copy.wait_recv()

    def forward(i, carry):
        rows = pl.ds(pl.multiple_of(OWN + i * 512, 512), 512)
        total = jnp.dot(dense[0, rows, :], xall[0], preferred_element_type=F32)
        total = total + jnp.dot(dense[1, rows, :], xall[1], preferred_element_type=F32)
        ymate[pl.ds(4 * i, 4)] = total.astype(BF16).reshape(4, TILE, HID)
        return carry

    lax.fori_loop(0, 2, forward, 0)
    swap_y = send(ymate, r_y, m_send, m_recv, mate)

    def forward_own(i, carry):
        rows = pl.ds(pl.multiple_of(i * 512, 512), 512)
        total = jnp.dot(dense[0, rows, :], xall[0], preferred_element_type=F32)
        total = total + jnp.dot(dense[1, rows, :], xall[1], preferred_element_type=F32)
        ys[pl.ds(4 * i, 4)] = total.astype(BF16).reshape(4, TILE, HID)
        return carry

    lax.fori_loop(0, 2, forward_own, 0)

    for d in (1, 7, 2, 6, 3, 5, 4):
        us[d].wait_recv()
        at = (z - d + NZ) % NZ
        vs.append(send(ut.at[at], ut.at[NZ + at], v_send.at[d], v_recv.at[d], mate))

    swap_y.wait_recv()
    for i in range(NZ):
        ys[i] = (ys[i].astype(F32) + r_y[i].astype(F32)).astype(BF16)
    fwd = [
        send(ys.at[(z + d) % NZ], r_fwd.at[d], y_send.at[d], y_recv.at[d], device((z + d) % NZ, yl, k, r))
        for d in Z_ORDER
    ]

    for copy in vs:
        copy.wait_recv()
    for i in range(2 * NZ):
        utw[:, i * TILE : (i + 1) * TILE] = ut[i]
    fs[0].wait_recv()
    other_rows = lax.rsqrt(dother[...].astype(F32))
    for c in range(2):
        ysd = (yl + c) % 2
        roots = root_rows if c == 0 else other_rows
        for xd in range(4):
            columns = slice(xd * 256, (xd + 1) * 256)
            prod = jnp.dot(utw[...], dense[c, :, columns], preferred_element_type=F32)
            root = jnp.concatenate([roots[2 * xd : 2 * xd + 1], roots[2 * xd + 1 : 2 * xd + 2]], axis=1)
            db[c, :, columns] = (prod * root).astype(BF16)
            prod = prod.astype(BF16)
            for h in range(2):
                piece = prod[:, h * TILE : (h + 1) * TILE]
                bt[0, xd, 2 * h + ysd] = piece[0:TILE, :]
                bt[1, 2 * h + ysd, xd] = piece[TILE:, :]

    up = (cot[...].astype(F32).T * own_root).astype(BF16).astype(F32)
    mine = pl.ds(pl.multiple_of(r * TILE, TILE), TILE)
    db[0, :, mine] = (db[0, :, mine].astype(F32) + up * own_root).astype(BF16)

    for copy in fs[1:]:
        copy.wait_recv()
    nt = (((1,), (1,)), ((), ()))
    part = lax.dot_general(feat[...], db[0], nt, preferred_element_type=F32)
    part = part + lax.dot_general(fother[...], db[1], nt, preferred_element_type=F32)
    for h in range(2):
        gp[h, 0:F_IN, :] = part[:, h * TILE : (h + 1) * TILE]
        gp[h, F_IN:F_PAD, :] = jnp.zeros((F_PAD - F_IN, TILE), F32)
    swap = send(gp.at[1 - k], r_swap, w_send, w_recv, mate)
    swap.wait_recv()
    gs[...] = (gp[k] + r_swap[...]).reshape(16, CHUNK, TILE)
    gsend[:, 0:CHUNK, :] = gs[...].astype(BF16)
    gsend[:, CHUNK:WIRE, :] = jnp.zeros((16, WIRE - CHUNK, TILE), BF16)

    planes = []
    for i in PLANE_ORDER:
        xd, yd = (x + i // 4) % 4, (y + i % 4) % 4
        planes.append(
            send(gsend.at[xd * 4 + yd], r_plane.at[i], g_send.at[i], g_recv.at[i], device_xy(z, k, xd, yd))
        )

    here = (x, y)
    ones = []
    for d in RING_ORDER:
        for h in range(2):
            at = (here[h] + d) % 4
            dev = device_xy(z, k, (x + d) % 4, y) if h == 0 else device_xy(z, k, x, (y + d) % 4)
            ones.append(send(bt.at[h, at], r_one.at[h, d], a_send.at[h, d], a_recv.at[h, d], dev))

    for copy in planes:
        copy.wait_recv()
    total = gs[spot]
    for i in range(1, 16):
        total = total + r_plane[i, 0:CHUNK, :].astype(F32)
    r_z[z] = jnp.concatenate([total, jnp.zeros((WIRE - CHUNK, TILE), F32)], axis=0).astype(BF16)
    zs = [
        send(r_z.at[z], r_z.at[z], z_send.at[d], z_recv.at[d], device((z + d) % NZ, yl, k, r)) for d in Z_ORDER
    ]

    for copy in ones:
        copy.wait_recv()
    twos = []
    for d in RING_ORDER + (0,):
        for h in range(2):
            at = (here[1 - h] + d) % 4
            total = bt[h, here[h], at].astype(F32)
            for e in range(1, 4):
                total = total + r_one[h, e, at].astype(F32)
            if d:
                p_part[h, d] = total.astype(BF16)
                dev = device_xy(z, k, x, (y + d) % 4) if h == 0 else device_xy(z, k, (x + d) % 4, y)
                twos.append(send(p_part.at[h, d], r_two.at[h, d], b_send.at[h, d], b_recv.at[h, d], dev))
            elif h == 0:
                top = total
            else:
                bottom = total

    for copy in zs:
        copy.wait_recv()
    total = r_z[0, 0:CHUNK, :].astype(F32)
    for i in range(1, NZ):
        total = total + r_z[i, 0:CHUNK, :].astype(F32)
    half = pl.ds(pl.multiple_of(k * TILE, TILE), TILE)
    gw[spot, :, half] = total * scale
    spread = []
    for i in PLANE_ORDER:
        xd, yd = (x + i // 4) % 4, (y + i % 4) % 4
        spread.append(
            send(gw.at[spot, :, half], gw.at[spot, :, half], h_send.at[i], h_recv.at[i], device_xy(z, k, xd, yd))
        )

    for copy in twos:
        copy.wait_recv()
    for e in range(1, 4):
        top = top + r_two[0, e].astype(F32)
        bottom = bottom + r_two[1, e].astype(F32)
    back = jnp.concatenate([top, bottom], axis=0) + up
    node_grad = (back * own_root).astype(BF16)
    gin[...] = jnp.dot(weight[...], node_grad, preferred_element_type=F32).astype(BF16)

    for copy in fwd:
        copy.wait_recv()
    total = ys[z].astype(F32) + xall[0, mine, :].astype(F32)
    for d in range(1, NZ):
        total = total + r_fwd[d].astype(F32)
    root_col = jnp.broadcast_to(own_root, (8, TILE)).T
    out[...] = (total * root_col[:, 0:1]).astype(BF16)

    last = [send(gw.at[spot, :, half], gw.at[spot, :, half], e_send.at[0], e_recv.at[0], mate)]
    for i, copy in reversed(list(zip(PLANE_ORDER, spread))):
        copy.wait_recv()
        at = ((x - i // 4 + 4) % 4) * 4 + (y - i % 4 + 4) % 4
        last.append(send(gw.at[at, :, half], gw.at[at, :, half], e_send.at[i], e_recv.at[i], mate))

    for j in range(4):
        _, mine, copy = code_copy(j)

        @pl.when(jnp.logical_not(mine))
        def _():
            copy.wait_send()

    for copy in last:
        copy.wait_recv()
    for copy in pending:
        copy.wait_send()


def layer_call(scale, feat, weight, deg, cot, codes, tiles):
    dma = pltpu.SemaphoreType.DMA
    vm = pltpu.VMEM
    i32 = jnp.int32
    scratch = [
        vm((16, WIRE, TILE), BF16), vm((F_IN, OWN), BF16), vm((4, 40, TILE), i32), vm((4, 40, TILE), i32), vm((8, 4, 8, TILE), i32), vm((32, 8, TILE), i32), vm((8, 8, TILE), i32), pltpu.SMEM((8, 8, TILE), i32),
        vm((4, 5, TILE, TILE), BF16), vm((2, 2 * OWN, OWN), BF16), vm((2, OWN, HID), BF16),
        vm((F_IN, OWN), BF16), vm((8, TILE), i32), vm((2 * NZ, HID, TILE), BF16),
        vm((HID, 2 * OWN), BF16), vm((2, HID, OWN), BF16),
        vm((NZ, TILE, HID), BF16), vm((NZ, TILE, HID), BF16), vm((NZ, TILE, HID), BF16), vm((NZ, TILE, HID), BF16),
        vm((2, 4, 4, TILE, TILE), BF16), vm((2, 4, 4, TILE, TILE), BF16),
        vm((2, 4, TILE, TILE), BF16), vm((2, 4, TILE, TILE), BF16),
        vm((2, F_PAD, TILE), F32), vm((F_PAD, TILE), F32), vm((16, CHUNK, TILE), F32), vm((16, WIRE, TILE), BF16),
        vm((NZ, WIRE, TILE), BF16),
        dma, dma((8,)), dma((4,)), dma((4,)), dma((8,)), dma((8,)), dma((4,)), dma((4,)),
        dma((8,)), dma((8,)), dma((8,)), dma((8,)), dma((2,)), dma((2,)), dma((4,)), dma((4,)),
        dma, dma, dma((8,)), dma((8,)), dma((2, 4)), dma((2, 4)), dma((2, 4)), dma((2, 4)),
        dma, dma, dma((16,)), dma((16,)), dma((8,)), dma((8,)), dma((16,)), dma((16,)), dma((16,)), dma((16,)),
    ]
    return pl.pallas_call(
        functools.partial(layer_kernel, scale),
        out_shape=(
            jax.ShapeDtypeStruct((TILE, HID), BF16),
            jax.ShapeDtypeStruct((F_IN, TILE), BF16),
            jax.ShapeDtypeStruct((16, CHUNK, HID), F32),
        ),
        in_specs=[pl.BlockSpec(memory_space=pl.ANY)] + [VM] * 5,
        out_specs=(VM, VM, VM),
        scratch_shapes=scratch,
        compiler_params=pltpu.CompilerParams(
            collective_id=0, has_side_effects=True, vmem_limit_bytes=VMEM_LIMIT
        ),
    )(feat, weight, deg, cot, codes, tiles)


def per_device(node_features, weight, degree, tile_index, edge_codes, cotangent):
    scale = 1.0 / math.sqrt(node_features.shape[0] * lax.axis_size("loop"))
    out, gin, gw = layer_call(
        scale, node_features.T, weight, degree.reshape(8, TILE), cotangent, edge_codes[0], tile_index[0]
    )
    return (out, gw.reshape(F_PAD, HID)[:F_IN], gin.T)


def solution(mesh):
    return jax.shard_map(
        per_device,
        mesh=mesh,
        in_specs=(
            P("loop", None),
            P(),
            P("loop"),
            P("loop", "rep", None),
            P("loop", "rep", None, None),
            P(("loop", "rep"), None),
        ),
        out_specs=(P(("loop", "rep"), None), P(), P(("loop", "rep"), None)),
        check_vma=False,
    )
```
